32 devices in a mesh: row: 8 (over y, x, core), col: 4 (over z).
Axes of the slice: x: 2, y: 2, z: 4, core: 2. Of those that a mesh axis runs over, the one named last changes fastest.
Arguments:
- ensemble: float32 [4096, 1024], P(('row', 'col')), may hold values from -6 to 6
- obs_rows: int32 [2, 256], replicated, may hold values from 0 to 127
- owner: int32 [2], replicated, may hold values from 0 to 7
- obs_value: float32 [2, 256], replicated, may hold values from -8 to 8
- obs_var: float32 [2, 256], replicated, may hold values from 0.1 to 2
- taper_mask: int32 [2, 32, 2], P(None, ('row', 'col')), may hold values 0 or 1
Outputs:
- analysis: float32 [4096, 1024], P(('row', 'col'))
The draws below stay inside these ranges and needn't reach their ends.
Inputs may be any that keep to these rules, and one draw needn't show every extreme that they name: `obs_rows`: observation p of batch b lies on the device at col index p // (256 / 4) of group owner[b]; batches may repeat a group and an observation may repeat a row.
All inputs are finite; a program needn't handle non-finite values. No bound on the sum of `taper_mask` on one device may be relied on, other than what follows from the above.
Results may differ from the reference program's by a relative error of at most 0.00018.
Values sent between devices are 32-bit elements; how exact they have to be, the bound alone decides.
A program may use at most 64 MiB of HBM per device.

```python
import math
import jax
import jax.numpy as jnp
from jax import lax

ROWS_DEV = 128
MEMBERS = 1024
OBS = 256
BATCHES = 2
BLK = 128
NSTATE = 4096
N_ROW = 8
N_COL = 4


def touch_ends(values, stream_key, smallest, largest):
    place = [jax.random.randint(jax.random.fold_in(stream_key, axis), (), 0, length) for axis, length in enumerate(values.shape)]
    longest = values.shape.index(max(values.shape))
    neighbour = place[:longest] + [(place[longest] + 1) % values.shape[longest]] + place[longest + 1:]
    return values.at[tuple(place)].set(smallest).at[tuple(neighbour)].set(largest)


def levels(key, shape, split, least, top_value):
    level = 1.0
    for position, parts in split:
        heights = jax.random.uniform(jax.random.fold_in(jax.random.fold_in(key, 6), position), (parts,), jnp.float32, least / len(split), top_value / len(split))
        level = level * jnp.repeat(jnp.exp(heights), shape[position] // parts).reshape((-1,) + (1,) * (len(shape) - 1 - position))
    return level


def noise(stream_key, shape, scale, limit, cuts=(), held_as=jnp.bfloat16):
    array = scale * jax.random.normal(stream_key, shape, jnp.float32)
    if cuts:
        array = array * levels(stream_key, shape, cuts, -0.22, 0.18)
    return jnp.clip(array, -limit, limit).astype(held_as)


def setup_inputs(seed: int = 0) -> dict:
    key_of = jax.random.split(jax.random.key(seed), 7)
    ensemble = noise(key_of[0], (NSTATE, MEMBERS), 1.0, 6.0, ((0, 32),), jnp.float32)
    obs_rows = touch_ends(jax.random.randint(key_of[1], (BATCHES, OBS), 0, ROWS_DEV), jax.random.fold_in(key_of[1], 1), 0, ROWS_DEV - 1).astype(jnp.int32)
    owner = jax.random.randint(key_of[2], (BATCHES,), 0, N_ROW).astype(jnp.int32)
    obs_value = noise(key_of[3], (BATCHES, OBS), 1.5, 8.0, (), jnp.float32)
    obs_var = jnp.clip(jnp.exp(jax.random.uniform(key_of[4], (BATCHES, OBS), jnp.float32, math.log(0.1), math.log(2.0))), 0.1, 2.0)
    taper_mask = touch_ends((jax.random.randint(key_of[5], (BATCHES, NSTATE // BLK, OBS // BLK), 0, 4) < 3).astype(jnp.int32), jax.random.fold_in(key_of[5], 1), 0, 1)
    return dict(ensemble=ensemble, obs_rows=obs_rows, owner=owner, obs_value=obs_value, obs_var=obs_var, taper_mask=taper_mask)


def invert_spd(cov):
    count = cov.shape[0]
    factor = jnp.linalg.cholesky(cov)
    ident = jnp.eye(count, dtype=cov.dtype)
    lower_inv = lax.linalg.triangular_solve(factor, ident, left_side=True, lower=True)
    return lax.linalg.triangular_solve(factor, lower_inv, left_side=True, lower=True, transpose_a=True)

def reference(ensemble, obs_rows, owner, obs_value, obs_var, taper_mask):
    total = ensemble.shape[0]
    members = ensemble.shape[1]
    count = obs_rows.shape[1]
    per_dev = count // N_COL
    local_len = total // 4
    positions = jnp.arange(total, dtype=jnp.int32)
    state = ensemble
    for batch in range(BATCHES):
        mean = jnp.mean(state, axis=1, keepdims=True)
        anom = state - mean
        column_of = (jnp.arange(count, dtype=jnp.int32) // per_dev).astype(jnp.int32)
        glob = ((owner[batch] * N_COL + column_of) * ROWS_DEV + obs_rows[batch]).astype(jnp.int32)
        obs_anom = anom[glob]
        obs_mean = mean[glob, 0]
        cov = jnp.dot(obs_anom, obs_anom.T, precision=lax.Precision.HIGHEST) / (members - 1.0)
        cov = cov + jnp.diag(obs_var[batch])
        cov_inv = invert_spd(cov)
        innov = obs_value[batch] - obs_mean
        blocks = jnp.repeat(jnp.repeat(taper_mask[batch], BLK, axis=0), BLK, axis=1)
        dist = jnp.abs(positions[:, None] - glob[None, :]).astype(jnp.float32)
        taper = blocks.astype(jnp.float32) * jnp.exp(-dist / jnp.float32(local_len))
        cross = jnp.dot(anom, obs_anom.T, precision=lax.Precision.HIGHEST) / (members - 1.0)
        gain = jnp.dot(taper * cross, cov_inv, precision=lax.Precision.HIGHEST)
        shift = jnp.dot(gain, innov[:, None], precision=lax.Precision.HIGHEST)
        change = jnp.dot(gain, obs_anom, precision=lax.Precision.HIGHEST)
        state = mean + shift + anom - 0.5 * change
    return state
```

```python
import functools

import jax
import jax.numpy as jnp
from jax import lax
from jax.experimental import pallas as pl
from jax.experimental.pallas import tpu as pltpu
from jax.sharding import PartitionSpec as P

W = 16
F32 = jnp.float32
BF16 = jnp.bfloat16
NN = (((1,), (0,)), ((), ()))
NT = (((1,), (1,)), ((), ()))
TN = (((0,), (0,)), ((), ()))


def split2(x):
    hi = x.astype(BF16)
    return hi, (x - hi.astype(F32)).astype(BF16)


def split3(x):
    hi = x.astype(BF16)
    rest = x - hi.astype(F32)
    mid = rest.astype(BF16)
    return hi, mid, (rest - mid.astype(F32)).astype(BF16)


def mm(a, b, dims):
    return lax.dot_general(a, b, dims, preferred_element_type=F32)


def dot3(a, b, dims):
    return mm(a[0], b[0], dims) + (mm(a[0], b[1], dims) + mm(a[1], b[0], dims))


def sweep_inverse(cov):
    size = cov.shape[0]
    lane = lax.broadcasted_iota(jnp.int32, (W, size), 1)
    row = lax.broadcasted_iota(jnp.int32, (W, size), 0)
    row_small = lax.broadcasted_iota(jnp.int32, (W, 128), 0)

    def body(k, carry):
        start = pl.multiple_of(k * W, W)
        panel = cov[pl.ds(start, W), :]
        rolled = pltpu.roll(panel, size - start, 1)
        cols = [jnp.broadcast_to(rolled[:, i:i + 1], (W, 128)) for i in range(W)]
        inside = (lane >= start) & (lane < start + W)
        left = jnp.where(inside, jnp.where(lane - start == row, -1.0, 0.0), panel)
        right = left
        scale = jnp.zeros((W, 128), F32)
        for j in range(W):
            inv = 1.0 / cols[j][j:j + 1, :]
            here = row_small == j
            mult = jnp.where(here, 0.0, cols[j])
            scale = jnp.where(here, inv, scale)
            for i in range(j + 1, W):
                cols[i] = cols[i] - mult * (cols[i][j:j + 1, :] * inv)
            wide = jnp.concatenate([mult] * (size // 128), axis=1)
            wide_inv = jnp.concatenate([inv] * (size // 128), axis=1)
            right = right - wide * (right[j:j + 1, :] * wide_inv)
        right = right * jnp.concatenate([scale] * (size // 128), axis=1)
        a1, a2, a3 = split3(left)
        b1, b2, b3 = split3(right)
        lhs = jnp.concatenate([a1, a1, a2, a1, a2, a3], axis=0)
        rhs = jnp.concatenate([b1, b2, b1, b3, b2, b1], axis=0)
        change = mm(lhs, rhs, TN)
        r_ids = lax.broadcasted_iota(jnp.int32, (size, size), 0)
        c_ids = lax.broadcasted_iota(jnp.int32, (size, size), 1)
        hit = ((r_ids >= start) & (r_ids < start + W)) | ((c_ids >= start) & (c_ids < start + W))
        cov[...] = jnp.where(hit, 0.0, cov[...]) - change
        return carry

    lax.fori_loop(0, size // W, body, 0)


def row_mean(x):
    return jnp.sum(x, axis=1, keepdims=True) * (1.0 / x.shape[1])


def covariance(anom2, var_ref, cov):
    size, members = anom2[0].shape
    r_ids = lax.broadcasted_iota(jnp.int32, (size, size), 0)
    c_ids = lax.broadcasted_iota(jnp.int32, (size, size), 1)
    full = dot3(anom2, anom2, NT) * (1.0 / (members - 1.0))
    cov[...] = full + jnp.where(r_ids == c_ids, jnp.broadcast_to(var_ref, (size, size)), 0.0)


def first_kernel(obs_ref, var_ref, out_ref):
    obs = obs_ref[...]
    covariance(split2(obs - row_mean(obs)), var_ref[...], out_ref)
    sweep_inverse(out_ref)


def taper_of(positions, glob, mask, local_len):
    dist = jnp.abs(positions - glob).astype(F32)
    return mask * jnp.exp(-dist / local_len)


def gain_step(anom2, obs2, neg_inv2, taper, members):
    cross = dot3(anom2, obs2, NT) * (1.0 / (members - 1.0))
    return dot3(split2(taper * cross), neg_inv2, NN)


def second_kernel(local_len, x_ref, g0_ref, g1_ref, inv_ref, glob_ref, gcol_ref, pos_ref, val_ref, var_ref,
                  mask0_ref, mask0g_ref, mask1_ref, out_ref, x1, g1, cov):
    members = x_ref.shape[1]
    rows = x_ref.shape[0]
    size = g0_ref.shape[0]
    g0 = g0_ref[...]
    m0 = row_mean(g0)
    a0 = g0 - m0
    a02 = split2(a0)
    inv2 = split2(inv_ref[...])
    push = split2(val_ref[:, 0:1] - m0 - 0.5 * a0)
    glob0 = glob_ref[0:1, :]
    glob1 = glob_ref[1:2, :]
    pos = pos_ref[...]
    for src, where, mask, dst in ((x_ref, pos, mask0_ref, x1), (g1_ref, gcol_ref[:, 1:2], mask0g_ref, g1)):
        x = src[...]
        taper = taper_of(where, glob0, mask[...], local_len)
        gain = split2(gain_step(split2(x - row_mean(x)), a02, inv2, taper, members))
        dst[...] = x - dot3(gain, push, NN)
    g = g1[...]
    m1 = row_mean(g)
    a1 = g - m1
    a12 = split2(a1)
    covariance(a12, var_ref[1:2, :], cov)
    sweep_inverse(cov)
    push = split2(val_ref[:, 1:2] - m1 - 0.5 * a1)
    x = x1[...]
    taper = taper_of(pos, glob1, mask1_ref[...], local_len)
    gain = split2(gain_step(split2(x - row_mean(x)), a12, split2(cov[...]), taper, members))
    out_ref[...] = x - dot3(gain, push, NN)


def on_device(ensemble, obs_rows, owner, obs_value, obs_var, taper_mask):
    rows, members = ensemble.shape
    batches, count = obs_rows.shape
    ncols = lax.axis_size("col")
    nrows = lax.axis_size("row")
    per_dev = count // ncols
    nblk = taper_mask.shape[2]
    local_len = float(rows * nrows * ncols // 4)
    my_row = lax.axis_index("row")
    my_col = lax.axis_index("col")
    first = (my_row * ncols + my_col) * rows
    row_ids = jnp.arange(rows, dtype=jnp.int32)
    column_of = jnp.arange(count, dtype=jnp.int32) // per_dev
    glob = (owner[:, None] * ncols + column_of[None, :]) * rows + obs_rows
    mine = lax.dynamic_slice_in_dim(obs_rows, my_col * per_dev, per_dev, axis=1)
    shared = []
    for batch in range(batches):
        here = (owner[batch] == my_row)
        picker = ((mine[batch][:, None] == row_ids[None, :]) & here).astype(F32)
        part = jnp.dot(picker, ensemble, precision=lax.Precision.HIGHEST)
        if batch == 1:
            note = jnp.where(here, taper_mask[0, 0].astype(F32), 0.0)
            note = jnp.pad(jnp.broadcast_to(note[None, :], (8, nblk)), ((0, 0), (0, members - nblk)))
            part = jnp.concatenate([part, note], axis=0)
        part = lax.psum(part, "row")
        shared.append(lax.all_gather(part, "col", axis=0))
    g0 = shared[0].reshape(count, members)
    g1 = shared[1][:, :per_dev].reshape(count, members)
    mask_g = jnp.repeat(shared[1][:, per_dev, :nblk], per_dev, axis=0)
    widen = lambda m: jnp.repeat(m.astype(F32), count // nblk, axis=-1)
    vmem = pl.BlockSpec(memory_space=pltpu.VMEM)
    inv = pl.pallas_call(
        first_kernel,
        out_shape=jax.ShapeDtypeStruct((count, count), F32),
        in_specs=[vmem] * 2,
        out_specs=vmem,
        compiler_params=pltpu.CompilerParams(vmem_limit_bytes=32 * 2**20),
        cost_estimate=pl.CostEstimate(flops=10**10, bytes_accessed=2**21, transcendentals=0),
    )(g0, obs_var[0:1])
    return pl.pallas_call(
        functools.partial(second_kernel, local_len),
        out_shape=jax.ShapeDtypeStruct((rows, members), F32),
        in_specs=[vmem] * 12,
        out_specs=vmem,
        scratch_shapes=[
            pltpu.VMEM((rows, members), F32),
            pltpu.VMEM((count, members), F32),
            pltpu.VMEM((count, count), F32),
        ],
        compiler_params=pltpu.CompilerParams(vmem_limit_bytes=40 * 2**20),
        cost_estimate=pl.CostEstimate(flops=2 * 10**10, bytes_accessed=2**22, transcendentals=0),
    )(
        ensemble, g0, g1, inv, glob, glob.T, (first + row_ids)[:, None], obs_value.T, obs_var,
        widen(taper_mask[0]), widen(mask_g), widen(taper_mask[1]),
    )


def solution(mesh):
    in_specs = (P(("row", "col"), None), P(), P(), P(), P(), P(None, ("row", "col"), None))
    out_specs = P(("row", "col"), None)
    return jax.shard_map(
        on_device, mesh=mesh, in_specs=in_specs, out_specs=out_specs, check_vma=False
    )
```

```python
import functools

import jax
import jax.numpy as jnp
from jax import lax
from jax.experimental import pallas as pl
from jax.experimental.pallas import tpu as pltpu
from jax.sharding import PartitionSpec as P

W = 16
F32 = jnp.float32
BF16 = jnp.bfloat16
NN = (((1,), (0,)), ((), ()))
NT = (((1,), (1,)), ((), ()))
TN = (((0,), (0,)), ((), ()))
MESH = pl.DeviceIdType.MESH
VMEM = pl.BlockSpec(memory_space=pltpu.VMEM)
SMEM = pl.BlockSpec(memory_space=pltpu.SMEM)


def split2(x):
    hi = x.astype(BF16)
    return hi, (x - hi.astype(F32)).astype(BF16)


def split3(x):
    hi = x.astype(BF16)
    rest = x - hi.astype(F32)
    mid = rest.astype(BF16)
    return hi, mid, (rest - mid.astype(F32)).astype(BF16)


def mm(a, b, dims):
    return lax.dot_general(a, b, dims, preferred_element_type=F32)


def dot3(a, b, dims):
    return mm(a[0], b[0], dims) + (mm(a[0], b[1], dims) + mm(a[1], b[0], dims))


def sweep_inverse(cov):
    size = cov.shape[0]
    lane = lax.broadcasted_iota(jnp.int32, (W, size), 1)
    row = lax.broadcasted_iota(jnp.int32, (W, size), 0)
    row_small = lax.broadcasted_iota(jnp.int32, (W, 128), 0)

    def body(k, carry):
        start = pl.multiple_of(k * W, W)
        panel = cov[pl.ds(start, W), :]
        rolled = pltpu.roll(panel, size - start, 1)
        cols = [jnp.broadcast_to(rolled[:, i:i + 1], (W, 128)) for i in range(W)]
        inside = (lane >= start) & (lane < start + W)
        left = jnp.where(inside, jnp.where(lane - start == row, -1.0, 0.0), panel)
        right = left
        scale = jnp.zeros((W, 128), F32)
        for j in range(W):
            inv = 1.0 / cols[j][j:j + 1, :]
            here = row_small == j
            mult = jnp.where(here, 0.0, cols[j])
            scale = jnp.where(here, inv, scale)
            for i in range(j + 1, W):
                cols[i] = cols[i] - mult * (cols[i][j:j + 1, :] * inv)
            wide = jnp.concatenate([mult] * (size // 128), axis=1)
            wide_inv = jnp.concatenate([inv] * (size // 128), axis=1)
            right = right - wide * (right[j:j + 1, :] * wide_inv)
        right = right * jnp.concatenate([scale] * (size // 128), axis=1)
        a1, a2, a3 = split3(left)
        b1, b2, b3 = split3(right)
        lhs = jnp.concatenate([a1, a1, a2, a1, a2, a3], axis=0)
        rhs = jnp.concatenate([b1, b2, b1, b3, b2, b1], axis=0)
        change = mm(lhs, rhs, TN)
        r_ids = lax.broadcasted_iota(jnp.int32, (size, size), 0)
        c_ids = lax.broadcasted_iota(jnp.int32, (size, size), 1)
        hit = ((r_ids >= start) & (r_ids < start + W)) | ((c_ids >= start) & (c_ids < start + W))
        cov[...] = jnp.where(hit, 0.0, cov[...]) - change
        return carry

    lax.fori_loop(0, size // W, body, 0)


def row_mean(x):
    return jnp.sum(x, axis=1, keepdims=True) * (1.0 / x.shape[1])


def covariance(anom2, var_ref, cov):
    size, members = anom2[0].shape
    r_ids = lax.broadcasted_iota(jnp.int32, (size, size), 0)
    c_ids = lax.broadcasted_iota(jnp.int32, (size, size), 1)
    full = dot3(anom2, anom2, NT) * (1.0 / (members - 1.0))
    cov[...] = full + jnp.where(r_ids == c_ids, jnp.broadcast_to(var_ref, (size, size)), 0.0)


def inverse_of(obs, var_row, cov):
    covariance(split2(obs - row_mean(obs)), var_row, cov)
    sweep_inverse(cov)


def first_kernel(obs_ref, var_ref, out_ref):
    inverse_of(obs_ref[...], var_ref[0:1, :], out_ref)


def share_kernel(nrows, ncols, x_ref, rows_ref, owner_ref, mask_ref, var_ref, g_ref, note_ref, inv_ref,
                 src, slots, note_src, note_slots, sum_s, sum_r, line_s, line_r, plane_s, plane_r, pair_s, pair_r,
                 nsum_s, nsum_r, nline_s, nline_r):
    me = lax.axis_index("row")
    col = lax.axis_index("col")
    nstate, members = x_ref.shape
    count = rows_ref.shape[1]
    per_dev = count // ncols
    q = per_dev // nrows
    half = nrows // 2
    sibling = me + 1 - 2 * (me % 2)

    barrier = pltpu.get_barrier_semaphore()
    for d in range(1, nrows):
        pl.semaphore_signal(barrier, inc=1, device_id=((me + d) % nrows, col), device_id_type=MESH)
    for d in range(1, ncols):
        pl.semaphore_signal(barrier, inc=1, device_id=(me, (col + d) % ncols), device_id_type=MESH)

    def put(source, target, send, recv, row, column):
        copy = pltpu.make_async_remote_copy(
            src_ref=source, dst_ref=target, send_sem=send, recv_sem=recv,
            device_id=(row, column), device_id_type=MESH)
        copy.start()
        return copy

    x3 = split3(x_ref[...])
    state_ids = lax.broadcasted_iota(jnp.int32, (nstate, per_dev), 0)
    sent = []

    def select(b):
        ids = jnp.broadcast_to(rows_ref[b:b + 1, :], (8, count))
        ids = pltpu.roll(ids, (count - col * per_dev) % count, 1)[0:1, :per_dev]
        here = jnp.full((1, per_dev), owner_ref[b], jnp.int32) == me
        ids = jnp.where(here, ids, -1)
        pick = jnp.where(ids == state_ids, 1.0, 0.0).astype(BF16)
        src[b] = (mm(pick, x3[0], TN) + mm(pick, x3[1], TN)) + mm(pick, x3[2], TN)

    def scatter(b):
        copies = []
        for d in range(1, nrows):
            peer = (me + d) % nrows
            copies.append(put(src.at[b, pl.ds(pl.multiple_of(peer * q, q), q)], slots.at[b, d - 1],
                              sum_s.at[b, d - 1], sum_r.at[b, d - 1], peer, col))
        sent.extend(copies)
        return copies

    def along_line(b, copies):
        for copy in copies:
            copy.wait_recv()
        total = src[b, pl.ds(pl.multiple_of(me * q, q), q), :]
        for d in range(1, nrows):
            total = total + slots[b, d - 1]
        g_ref[b, col, me] = total
        mine = g_ref.at[b, col, me]
        copies = [put(mine, mine, line_s.at[b, d - 1], line_r.at[b, d - 1], me, (col + d) % ncols)
                  for d in range(1, ncols)]
        sent.extend(copies)
        return copies

    def spread(b, d):
        slab = g_ref.at[b, (col + ncols - d) % ncols, me]
        copies = [put(slab, slab, plane_s.at[b, d, c - 1], plane_r.at[b, d, c - 1], (me + 2 * c) % nrows, col)
                  for c in range(1, half)]
        pairs = [put(slab, slab, pair_s.at[b, d, 0], pair_r.at[b, d, 0], sibling, col)]
        sent.extend(copies + pairs)
        return copies, pairs

    def in_plane(b, lines, first):
        planes, pairs = [first[0]], list(first[1])
        for d in range(1, ncols):
            lines[d - 1].wait_recv()
            more = spread(b, d)
            planes.append(more[0])
            pairs.extend(more[1])
        return planes, pairs

    def in_chip(b, planes, pairs):
        for d in range(ncols):
            for c in range(1, half):
                planes[d][c - 1].wait_recv()
                slab = g_ref.at[b, (col + ncols - d) % ncols, (me + nrows - 2 * c) % nrows]
                pairs.append(put(slab, slab, pair_s.at[b, d, c], pair_r.at[b, d, c], sibling, col))
                sent.append(pairs[-1])
        for copy in pairs:
            copy.wait_recv()

    lane = lax.broadcasted_iota(jnp.int32, (8, 128), 1)
    note = jnp.zeros((8, 128), F32)
    for j in range(mask_ref.shape[2]):
        note = jnp.where(lane == j, mask_ref[0, 0, j].astype(F32), note)
    here = jnp.full((8, 128), owner_ref[1], jnp.int32) == me
    note_src[...] = jnp.where(here, note, 0.0)
    select(0)
    pl.semaphore_wait(barrier, nrows + ncols - 2)
    sums0 = scatter(0)
    select(1)
    lines0 = along_line(0, sums0)
    first0 = spread(0, 0)
    notes = [put(note_src, note_slots.at[d - 1], nsum_s.at[d - 1], nsum_r.at[d - 1], (me + d) % nrows, col)
             for d in range(1, nrows)]
    planes0, pairs0 = in_plane(0, lines0, first0)
    sums1 = scatter(1)
    in_chip(0, planes0, pairs0)

    lines1 = along_line(1, sums1)
    first1 = spread(1, 0)
    total = note_src[...]
    for d in range(1, nrows):
        notes[d - 1].wait_recv()
        total = total + note_slots[d - 1]
    note_ref[col] = total
    note_lines = [put(note_ref.at[col], note_ref.at[col], nline_s.at[d - 1], nline_r.at[d - 1], me, (col + d) % ncols)
                  for d in range(1, ncols)]
    obs = g_ref[0].reshape(count, members)
    covariance(split2(obs - row_mean(obs)), var_ref[0:1, :], inv_ref)
    planes1, pairs1 = in_plane(1, lines1, first1)
    sweep_inverse(inv_ref)
    in_chip(1, planes1, pairs1)
    for copy in note_lines:
        copy.wait_recv()
    for copy in sent + notes + note_lines:
        copy.wait_send()


def column_of(row, eye):
    return jnp.sum(jnp.where(eye, jnp.broadcast_to(row, eye.shape), 0.0), axis=1, keepdims=True)


def gain_step(anom2, obs2, neg_inv2, taper, members):
    cross = dot3(anom2, obs2, NT) * (1.0 / (members - 1.0))
    return dot3(split2(taper * cross), neg_inv2, NN)


def second_kernel(nrows, ncols, x_ref, g_ref, inv_ref, note_ref, rows_ref, owner_ref, val_ref, var_ref, mask_ref,
                  out_ref, x1, g1, cov):
    rows, members = x_ref.shape
    count = rows_ref.shape[1]
    per_dev = count // ncols
    nblk = mask_ref.shape[2]
    wide = count // nblk
    local_len = float(rows * nrows * ncols // 4)
    eye = (lax.broadcasted_iota(jnp.int32, (count, count), 0)
           == lax.broadcasted_iota(jnp.int32, (count, count), 1))
    lane = lax.broadcasted_iota(jnp.int32, (1, count), 1)
    device = jnp.zeros((1, count), jnp.int32)
    for c in range(1, ncols):
        device = device + jnp.where(lane >= c * per_dev, 1, 0)
    glob = [((owner_ref[b] * ncols + device) * rows + rows_ref[b:b + 1, :]).astype(F32) for b in range(2)]
    first = (lax.axis_index("row") * ncols + lax.axis_index("col")) * rows
    pos = (first + lax.broadcasted_iota(jnp.int32, (rows, count), 0)).astype(F32)

    def widen(values):
        out = jnp.zeros((1, count), F32)
        for j, value in enumerate(values):
            out = jnp.where((lane >= j * wide) & (lane < (j + 1) * wide), value, out)
        return out

    def taper_of(position, where, mask):
        return mask * jnp.exp(-jnp.abs(position - where) / local_len)

    mask = [widen([mask_ref[b, 0, j].astype(F32) for j in range(nblk)]) for b in range(2)]
    mask_g = jnp.concatenate(
        [jnp.broadcast_to(widen([note_ref[c, 0:1, j:j + 1] for j in range(nblk)]), (per_dev, count))
         for c in range(ncols)], axis=0)
    gcol = column_of(glob[1], eye)

    g0 = g_ref[0].reshape(count, members)
    m0 = row_mean(g0)
    a0 = g0 - m0
    a02 = split2(a0)
    inv2 = split2(inv_ref[...])
    push = split2(column_of(val_ref[0:1, :], eye) - m0 - 0.5 * a0)
    for src, where, held, dst in ((g_ref[1].reshape(count, members), gcol, mask_g, g1),
                                  (x_ref[...], pos, mask[0], x1)):
        taper = taper_of(where, glob[0], held)
        gain = split2(gain_step(split2(src - row_mean(src)), a02, inv2, taper, members))
        dst[...] = src - dot3(gain, push, NN)
    g = g1[...]
    m1 = row_mean(g)
    a1 = g - m1
    a12 = split2(a1)
    covariance(a12, var_ref[1:2, :], cov)
    sweep_inverse(cov)
    push = split2(column_of(val_ref[1:2, :], eye) - m1 - 0.5 * a1)
    x = x1[...]
    taper = taper_of(pos, glob[1], mask[1])
    gain = split2(gain_step(split2(x - row_mean(x)), a12, split2(cov[...]), taper, members))
    out_ref[...] = x - dot3(gain, push, NN)


def shared_by_collectives(ensemble, obs_rows, owner, taper_mask, ncols):
    rows, members = ensemble.shape
    batches, count = obs_rows.shape
    per_dev = count // ncols
    nblk = taper_mask.shape[2]
    my_row = lax.axis_index("row")
    mine = lax.dynamic_slice_in_dim(obs_rows, lax.axis_index("col") * per_dev, per_dev, axis=1)
    row_ids = jnp.arange(rows, dtype=jnp.int32)
    shared = []
    for batch in range(batches):
        here = owner[batch] == my_row
        picker = ((mine[batch][:, None] == row_ids[None, :]) & here).astype(F32)
        part = jnp.dot(picker, ensemble, precision=lax.Precision.HIGHEST)
        shared.append(lax.all_gather(lax.psum(part, "row"), "col", axis=0).reshape(count, members))
    note = jnp.where(owner[1] == my_row, taper_mask[0, 0].astype(F32), 0.0)
    note = jnp.pad(jnp.broadcast_to(note[None, :], (8, nblk)), ((0, 0), (0, 128 - nblk)))
    note = lax.all_gather(lax.psum(note, "row"), "col", axis=0)
    return jnp.stack(shared), note


def on_device(nrows, ncols, ensemble, obs_rows, owner, obs_value, obs_var, taper_mask):
    rows, members = ensemble.shape
    batches, count = obs_rows.shape
    per_dev = count // ncols
    inv_shape = jax.ShapeDtypeStruct((count, count), F32)
    if per_dev % (8 * nrows) == 0 and nrows % 2 == 0:
        q = per_dev // nrows
        half = nrows // 2
        dma = pltpu.SemaphoreType.DMA
        shared, note, inv = pl.pallas_call(
            functools.partial(share_kernel, nrows, ncols),
            out_shape=(
                jax.ShapeDtypeStruct((batches, ncols, nrows, q, members), F32),
                jax.ShapeDtypeStruct((ncols, 8, 128), F32),
                inv_shape,
            ),
            in_specs=[VMEM, VMEM, SMEM, SMEM, VMEM],
            out_specs=(VMEM, VMEM, VMEM),
            scratch_shapes=[
                pltpu.VMEM((batches, per_dev, members), F32),
                pltpu.VMEM((batches, nrows - 1, q, members), F32),
                pltpu.VMEM((8, 128), F32),
                pltpu.VMEM((nrows - 1, 8, 128), F32),
            ] + [dma((batches, nrows - 1))] * 2 + [dma((batches, ncols - 1))] * 2
            + [dma((batches, ncols, half - 1))] * 2 + [dma((batches, ncols, half))] * 2
            + [dma((nrows - 1,))] * 2 + [dma((ncols - 1,))] * 2,
            compiler_params=pltpu.CompilerParams(
                vmem_limit_bytes=40 * 2**20, collective_id=0, has_side_effects=True),
        )(ensemble, obs_rows, owner, taper_mask, obs_var)
    else:
        shared, note = shared_by_collectives(ensemble, obs_rows, owner, taper_mask, ncols)
        inv = pl.pallas_call(
            first_kernel,
            out_shape=inv_shape,
            in_specs=[VMEM] * 2,
            out_specs=VMEM,
            compiler_params=pltpu.CompilerParams(vmem_limit_bytes=40 * 2**20),
        )(shared[0], obs_var)
    return pl.pallas_call(
        functools.partial(second_kernel, nrows, ncols),
        out_shape=jax.ShapeDtypeStruct((rows, members), F32),
        in_specs=[VMEM] * 5 + [SMEM, VMEM, VMEM, SMEM],
        out_specs=VMEM,
        scratch_shapes=[
            pltpu.VMEM((rows, members), F32),
            pltpu.VMEM((count, members), F32),
            pltpu.VMEM((count, count), F32),
        ],
        compiler_params=pltpu.CompilerParams(vmem_limit_bytes=40 * 2**20),
    )(ensemble, shared, inv, note, obs_rows, owner, obs_value, obs_var, taper_mask)


def solution(mesh):
    in_specs = (P(("row", "col"), None), P(), P(), P(), P(), P(None, ("row", "col"), None))
    out_specs = P(("row", "col"), None)
    return jax.shard_map(
        functools.partial(on_device, mesh.shape["row"], mesh.shape["col"]),
        mesh=mesh, in_specs=in_specs, out_specs=out_specs, check_vma=False
    )
```

```python
import functools

import jax
import jax.numpy as jnp
from jax import lax
from jax.experimental import pallas as pl
from jax.experimental.pallas import tpu as pltpu
from jax.sharding import PartitionSpec as P

W = 16
F32 = jnp.float32
BF16 = jnp.bfloat16
NN = (((1,), (0,)), ((), ()))
NT = (((1,), (1,)), ((), ()))
TN = (((0,), (0,)), ((), ()))
MESH = pl.DeviceIdType.MESH
VMEM = pl.BlockSpec(memory_space=pltpu.VMEM)
SMEM = pl.BlockSpec(memory_space=pltpu.SMEM)
HBM = pl.BlockSpec(memory_space=pltpu.HBM)


def split2(x):
    hi = x.astype(BF16)
    return hi, (x - hi.astype(F32)).astype(BF16)


def split3(x):
    hi = x.astype(BF16)
    rest = x - hi.astype(F32)
    mid = rest.astype(BF16)
    return hi, mid, (rest - mid.astype(F32)).astype(BF16)


def mm(a, b, dims):
    return lax.dot_general(a, b, dims, preferred_element_type=F32)


def dot3(a, b, dims):
    return mm(a[0], b[0], dims) + (mm(a[0], b[1], dims) + mm(a[1], b[0], dims))


def sweep_inverse(cov, begin=0, end=None):
    size = cov.shape[0]
    lane = lax.broadcasted_iota(jnp.int32, (W, size), 1)
    row = lax.broadcasted_iota(jnp.int32, (W, size), 0)
    row_small = lax.broadcasted_iota(jnp.int32, (W, 128), 0)

    def body(k, carry):
        start = pl.multiple_of(k * W, W)
        panel = cov[pl.ds(start, W), :]
        rolled = pltpu.roll(panel, size - start, 1)
        cols = [jnp.broadcast_to(rolled[:, i:i + 1], (W, 128)) for i in range(W)]
        inside = (lane >= start) & (lane < start + W)
        left = jnp.where(inside, jnp.where(lane - start == row, -1.0, 0.0), panel)
        right = left
        scale = jnp.zeros((W, 128), F32)
        for j in range(W):
            inv = 1.0 / cols[j][j:j + 1, :]
            here = row_small == j
            mult = jnp.where(here, 0.0, cols[j])
            scale = jnp.where(here, inv, scale)
            for i in range(j + 1, W):
                cols[i] = cols[i] - mult * (cols[i][j:j + 1, :] * inv)
            wide = jnp.concatenate([mult] * (size // 128), axis=1)
            wide_inv = jnp.concatenate([inv] * (size // 128), axis=1)
            right = right - wide * (right[j:j + 1, :] * wide_inv)
        right = right * jnp.concatenate([scale] * (size // 128), axis=1)
        a1, a2, a3 = split3(left)
        b1, b2, b3 = split3(right)
        lhs = jnp.concatenate([a1, a1, a2, a1, a2, a3], axis=0)
        rhs = jnp.concatenate([b1, b2, b1, b3, b2, b1], axis=0)
        change = mm(lhs, rhs, TN)
        r_ids = lax.broadcasted_iota(jnp.int32, (size, size), 0)
        c_ids = lax.broadcasted_iota(jnp.int32, (size, size), 1)
        hit = ((r_ids >= start) & (r_ids < start + W)) | ((c_ids >= start) & (c_ids < start + W))
        cov[...] = jnp.where(hit, 0.0, cov[...]) - change
        return carry

    lax.fori_loop(begin, size // W if end is None else end, body, 0)


def row_mean(x):
    return jnp.sum(x, axis=1, keepdims=True) * (1.0 / x.shape[1])


def covariance(anom2, var_ref, cov):
    size, members = anom2[0].shape
    r_ids = lax.broadcasted_iota(jnp.int32, (size, size), 0)
    c_ids = lax.broadcasted_iota(jnp.int32, (size, size), 1)
    full = dot3(anom2, anom2, NT) * (1.0 / (members - 1.0))
    cov[...] = full + jnp.where(r_ids == c_ids, jnp.broadcast_to(var_ref, (size, size)), 0.0)


def column_of(row, eye):
    return jnp.sum(jnp.where(eye, jnp.broadcast_to(row, eye.shape), 0.0), axis=1, keepdims=True)


def eye_of(count):
    return (lax.broadcasted_iota(jnp.int32, (count, count), 0)
            == lax.broadcasted_iota(jnp.int32, (count, count), 1))


def widen(values, count):
    lane = lax.broadcasted_iota(jnp.int32, (1, count), 1)
    wide = count // len(values)
    out = jnp.zeros((1, count), F32)
    for j, value in enumerate(values):
        out = jnp.where((lane >= j * wide) & (lane < (j + 1) * wide), value, out)
    return out


def taper_of(position, where, mask, local_len):
    return mask * jnp.exp(-jnp.abs(position - where) / local_len)


def my_positions(rows, count, ncols):
    first = (lax.axis_index("row") * ncols + lax.axis_index("col")) * rows
    return (first + lax.broadcasted_iota(jnp.int32, (rows, count), 0)).astype(F32)


def gain_of(anom2, obs2, neg_inv2, taper, members):
    cross = dot3(anom2, obs2, NT) * (1.0 / (members - 1.0))
    return split2(dot3(split2(taper * cross), neg_inv2, NN))


def first_batch(nrows, ncols, g_ref, x_ref, rows_ref, owner_ref, mask_ref, val_ref, var_ref,
                inv_ref, x1_ref, anom_hi, anom_lo, push_hi, push_lo, aux_ref, beside):
    rows, members = x_ref.shape
    count = rows_ref.shape[1]
    nblk = mask_ref.shape[2]
    local_len = float(rows * nrows * ncols // 4)
    g0 = g_ref[0].reshape(count, members)
    m0 = row_mean(g0)
    a0 = g0 - m0
    anom_hi[...], anom_lo[...] = split2(a0)
    covariance((anom_hi[...], anom_lo[...]), var_ref[0:1, :], inv_ref)
    beside(0)
    lane = lax.broadcasted_iota(jnp.int32, (1, count), 1)
    device = jnp.zeros((1, count), jnp.int32)
    for c in range(1, ncols):
        device = device + jnp.where(lane >= c * (count // ncols), 1, 0)
    for b in range(2):
        aux_ref[b:b + 1, :] = ((owner_ref[b] * ncols + device) * rows + rows_ref[b:b + 1, :]).astype(F32)
        aux_ref[2 + b:3 + b, :] = widen([mask_ref[b, 0, j].astype(F32) for j in range(nblk)], count)
    aux_ref[4:6, :] = val_ref[...]
    aux_ref[6:8, :] = var_ref[...]
    push_hi[...], push_lo[...] = split2(column_of(val_ref[0:1, :], eye_of(count)) - m0 - 0.5 * a0)
    mid = 3 * (count // W) // 4
    sweep_inverse(inv_ref, 0, mid)
    beside(1)
    sweep_inverse(inv_ref, mid)
    x = x_ref[...]
    taper = taper_of(my_positions(rows, count, ncols), aux_ref[0:1, :], aux_ref[2:3, :], local_len)
    gain = gain_of(split2(x - row_mean(x)), (anom_hi[...], anom_lo[...]), split2(inv_ref[...]), taper, members)
    x1_ref[...] = x - dot3(gain, (push_hi[...], push_lo[...]), NN)
    beside(2)


def solo_kernel(nrows, ncols, *refs):
    first_batch(nrows, ncols, *refs, lambda stage: None)


def share_kernel(nrows, ncols, x_hbm, rows_hbm, owner_hbm, mask_hbm, val_hbm, var_hbm, g_ref, note_ref,
                 inv_ref, x1_ref, anom_hi, anom_lo, push_hi, push_lo, aux_ref,
                 x_ref, rows_ref, owner_ref, mask_ref, val_ref, var_ref, load, src, slots, note_src, note_slots, sum_s, sum_r, line_s, line_r, plane_s, plane_r, pair_s, pair_r,
                 nsum_s, nsum_r, nline_s, nline_r):
    loads = [pltpu.make_async_copy(source, target, load.at[k]) for k, (source, target) in enumerate((
        (x_hbm, x_ref), (rows_hbm, rows_ref), (owner_hbm, owner_ref), (mask_hbm, mask_ref),
        (val_hbm, val_ref), (var_hbm, var_ref)))]
    for copy in loads:
        copy.start()
    me = lax.axis_index("row")
    col = lax.axis_index("col")
    nstate, members = x_ref.shape
    count = rows_ref.shape[1]
    per_dev = count // ncols
    q = per_dev // nrows
    half = nrows // 2
    sibling = me + 1 - 2 * (me % 2)

    barrier = pltpu.get_barrier_semaphore()
    for d in range(1, nrows):
        pl.semaphore_signal(barrier, inc=1, device_id=((me + d) % nrows, col), device_id_type=MESH)
    for d in range(1, ncols):
        pl.semaphore_signal(barrier, inc=1, device_id=(me, (col + d) % ncols), device_id_type=MESH)

    def put(source, target, send, recv, row, column):
        copy = pltpu.make_async_remote_copy(
            src_ref=source, dst_ref=target, send_sem=send, recv_sem=recv,
            device_id=(row, column), device_id_type=MESH)
        copy.start()
        return copy

    for copy in loads:
        copy.wait()
    x3 = split3(x_ref[...])
    state_ids = lax.broadcasted_iota(jnp.int32, (nstate, per_dev), 0)
    sent = []

    def select(b):
        ids = jnp.broadcast_to(rows_ref[b:b + 1, :], (8, count))
        ids = pltpu.roll(ids, (count - col * per_dev) % count, 1)[0:1, :per_dev]
        here = jnp.full((1, per_dev), owner_ref[b], jnp.int32) == me
        ids = jnp.where(here, ids, -1)
        pick = jnp.where(ids == state_ids, 1.0, 0.0).astype(BF16)
        src[b] = (mm(pick, x3[0], TN) + mm(pick, x3[1], TN)) + mm(pick, x3[2], TN)

    def scatter(b):
        copies = []
        for d in range(1, nrows):
            peer = (me + d) % nrows
            copies.append(put(src.at[b, pl.ds(pl.multiple_of(peer * q, q), q)], slots.at[b, d - 1],
                              sum_s.at[b, d - 1], sum_r.at[b, d - 1], peer, col))
        sent.extend(copies)
        return copies

    def along_line(b, copies):
        for copy in copies:
            copy.wait_recv()
        total = src[b, pl.ds(pl.multiple_of(me * q, q), q), :]
        for d in range(1, nrows):
            total = total + slots[b, d - 1]
        g_ref[b, col, me] = total
        mine = g_ref.at[b, col, me]
        copies = [put(mine, mine, line_s.at[b, d - 1], line_r.at[b, d - 1], me, (col + d) % ncols)
                  for d in range(1, ncols)]
        sent.extend(copies)
        return copies

    def spread(b, d):
        slab = g_ref.at[b, (col + ncols - d) % ncols, me]
        copies = [put(slab, slab, plane_s.at[b, d, c - 1], plane_r.at[b, d, c - 1], (me + 2 * c) % nrows, col)
                  for c in range(1, half)]
        pairs = [put(slab, slab, pair_s.at[b, d, 0], pair_r.at[b, d, 0], sibling, col)]
        sent.extend(copies + pairs)
        return copies, pairs

    def in_plane(b, lines, first):
        planes, pairs = [first[0]], list(first[1])
        for d in range(1, ncols):
            lines[d - 1].wait_recv()
            more = spread(b, d)
            planes.append(more[0])
            pairs.extend(more[1])
        return planes, pairs

    def in_chip(b, planes, pairs):
        hand_on(b, planes, pairs)
        for copy in pairs:
            copy.wait_recv()

    def hand_on(b, planes, pairs):
        for d in range(ncols):
            for c in range(1, half):
                planes[d][c - 1].wait_recv()
                slab = g_ref.at[b, (col + ncols - d) % ncols, (me + nrows - 2 * c) % nrows]
                pairs.append(put(slab, slab, pair_s.at[b, d, c], pair_r.at[b, d, c], sibling, col))
                sent.append(pairs[-1])

    lane = lax.broadcasted_iota(jnp.int32, (8, 128), 1)
    note = jnp.zeros((8, 128), F32)
    for j in range(mask_ref.shape[2]):
        note = jnp.where(lane == j, mask_ref[0, 0, j].astype(F32), note)
    here = jnp.full((8, 128), owner_ref[1], jnp.int32) == me
    note_src[...] = jnp.where(here, note, 0.0)
    select(0)
    pl.semaphore_wait(barrier, nrows + ncols - 2)
    sums0 = scatter(0)
    select(1)
    lines0 = along_line(0, sums0)
    first0 = spread(0, 0)
    notes = [put(note_src, note_slots.at[d - 1], nsum_s.at[d - 1], nsum_r.at[d - 1], (me + d) % nrows, col)
             for d in range(1, nrows)]
    planes0, pairs0 = in_plane(0, lines0, first0)
    sums1 = scatter(1)
    in_chip(0, planes0, pairs0)

    lines1 = along_line(1, sums1)
    first1 = spread(1, 0)
    total = note_src[...]
    for d in range(1, nrows):
        notes[d - 1].wait_recv()
        total = total + note_slots[d - 1]
    note_ref[col] = total
    note_lines = [put(note_ref.at[col], note_ref.at[col], nline_s.at[d - 1], nline_r.at[d - 1], me, (col + d) % ncols)
                  for d in range(1, ncols)]
    later = []

    def beside(stage):
        if stage == 0:
            later.extend(in_plane(1, lines1, first1))
        elif stage == 1:
            hand_on(1, *later)
        else:
            for copy in later[1] + note_lines:
                copy.wait_recv()

    first_batch(nrows, ncols, g_ref, x_ref, rows_ref, owner_ref, mask_ref, val_ref, var_ref,
                inv_ref, x1_ref, anom_hi, anom_lo, push_hi, push_lo, aux_ref, beside)
    for copy in sent + notes + note_lines:
        copy.wait_send()


def second_kernel(nrows, ncols, nblk, g_ref, note_ref, inv_ref, x1_ref, anom_hi, anom_lo, push_hi, push_lo, aux_ref,
                  out_ref, g1, cov):
    rows, members = x1_ref.shape
    count = inv_ref.shape[0]
    local_len = float(rows * nrows * ncols // 4)
    eye = eye_of(count)
    mask_g = jnp.concatenate(
        [jnp.broadcast_to(widen([note_ref[c, 0:1, j:j + 1] for j in range(nblk)], count), (count // ncols, count))
         for c in range(ncols)], axis=0)
    taper = taper_of(column_of(aux_ref[1:2, :], eye), aux_ref[0:1, :], mask_g, local_len)
    g = g_ref[1].reshape(count, members)
    gain = gain_of(split2(g - row_mean(g)), (anom_hi[...], anom_lo[...]), split2(inv_ref[...]), taper, members)
    g1[...] = g - dot3(gain, (push_hi[...], push_lo[...]), NN)
    g = g1[...]
    m1 = row_mean(g)
    a1 = g - m1
    a12 = split2(a1)
    covariance(a12, aux_ref[7:8, :], cov)
    sweep_inverse(cov)
    push = split2(column_of(aux_ref[5:6, :], eye) - m1 - 0.5 * a1)
    x = x1_ref[...]
    taper = taper_of(my_positions(rows, count, ncols), aux_ref[1:2, :], aux_ref[3:4, :], local_len)
    gain = gain_of(split2(x - row_mean(x)), a12, split2(cov[...]), taper, members)
    out_ref[...] = x - dot3(gain, push, NN)


def shared_by_collectives(ensemble, obs_rows, owner, taper_mask, ncols):
    rows, members = ensemble.shape
    batches, count = obs_rows.shape
    per_dev = count // ncols
    nblk = taper_mask.shape[2]
    my_row = lax.axis_index("row")
    mine = lax.dynamic_slice_in_dim(obs_rows, lax.axis_index("col") * per_dev, per_dev, axis=1)
    row_ids = jnp.arange(rows, dtype=jnp.int32)
    shared = []
    for batch in range(batches):
        here = owner[batch] == my_row
        picker = ((mine[batch][:, None] == row_ids[None, :]) & here).astype(F32)
        part = jnp.dot(picker, ensemble, precision=lax.Precision.HIGHEST)
        shared.append(lax.all_gather(lax.psum(part, "row"), "col", axis=0).reshape(count, members))
    note = jnp.where(owner[1] == my_row, taper_mask[0, 0].astype(F32), 0.0)
    note = jnp.pad(jnp.broadcast_to(note[None, :], (8, nblk)), ((0, 0), (0, 128 - nblk)))
    note = lax.all_gather(lax.psum(note, "row"), "col", axis=0)
    return jnp.stack(shared), note


def on_device(nrows, ncols, ensemble, obs_rows, owner, obs_value, obs_var, taper_mask):
    rows, members = ensemble.shape
    batches, count = obs_rows.shape
    per_dev = count // ncols
    half_shape = jax.ShapeDtypeStruct((count, members), BF16)
    kept = (
        jax.ShapeDtypeStruct((count, count), F32),
        jax.ShapeDtypeStruct((rows, members), F32),
        half_shape, half_shape, half_shape, half_shape,
        jax.ShapeDtypeStruct((8, count), F32),
    )
    limit = 40 * 2**20
    if per_dev % (8 * nrows) == 0 and nrows % 2 == 0:
        q = per_dev // nrows
        half = nrows // 2
        dma = pltpu.SemaphoreType.DMA
        shared, note, *held = pl.pallas_call(
            functools.partial(share_kernel, nrows, ncols),
            out_shape=(
                jax.ShapeDtypeStruct((batches, ncols, nrows, q, members), F32),
                jax.ShapeDtypeStruct((ncols, 8, 128), F32),
            ) + kept,
            in_specs=[HBM] * 6,
            out_specs=(VMEM,) * 9,
            scratch_shapes=[
                pltpu.VMEM(ensemble.shape, F32),
                pltpu.VMEM(obs_rows.shape, jnp.int32),
                pltpu.SMEM(owner.shape, jnp.int32),
                pltpu.SMEM(taper_mask.shape, jnp.int32),
                pltpu.VMEM(obs_value.shape, F32),
                pltpu.VMEM(obs_var.shape, F32),
                dma((6,)),
                pltpu.VMEM((batches, per_dev, members), F32),
                pltpu.VMEM((batches, nrows - 1, q, members), F32),
                pltpu.VMEM((8, 128), F32),
                pltpu.VMEM((nrows - 1, 8, 128), F32),
            ] + [dma((batches, nrows - 1))] * 2 + [dma((batches, ncols - 1))] * 2
            + [dma((batches, ncols, half - 1))] * 2 + [dma((batches, ncols, half))] * 2
            + [dma((nrows - 1,))] * 2 + [dma((ncols - 1,))] * 2,
            compiler_params=pltpu.CompilerParams(
                vmem_limit_bytes=limit, collective_id=0, has_side_effects=True),
        )(*[pltpu.with_memory_space_constraint(arg, pltpu.HBM)
            for arg in (ensemble, obs_rows, owner, taper_mask, obs_value, obs_var)])
    else:
        shared, note = shared_by_collectives(ensemble, obs_rows, owner, taper_mask, ncols)
        held = pl.pallas_call(
            functools.partial(solo_kernel, nrows, ncols),
            out_shape=kept,
            in_specs=[VMEM] * 3 + [SMEM] * 2 + [VMEM] * 2,
            out_specs=(VMEM,) * 7,
            compiler_params=pltpu.CompilerParams(vmem_limit_bytes=limit),
        )(shared, ensemble, obs_rows, owner, taper_mask, obs_value, obs_var)
    return pl.pallas_call(
        functools.partial(second_kernel, nrows, ncols, taper_mask.shape[2]),
        out_shape=jax.ShapeDtypeStruct((rows, members), F32),
        in_specs=[VMEM] * 9,
        out_specs=VMEM,
        scratch_shapes=[pltpu.VMEM((count, members), F32), pltpu.VMEM((count, count), F32)],
        compiler_params=pltpu.CompilerParams(vmem_limit_bytes=limit),
    )(shared, note, *held)


def solution(mesh):
    in_specs = (P(("row", "col"), None), P(), P(), P(), P(), P(None, ("row", "col"), None))
    out_specs = P(("row", "col"), None)
    return jax.shard_map(
        functools.partial(on_device, mesh.shape["row"], mesh.shape["col"]),
        mesh=mesh, in_specs=in_specs, out_specs=out_specs, check_vma=False
    )
```

```python
import functools

import jax
import jax.numpy as jnp
from jax import lax
from jax.experimental import pallas as pl
from jax.experimental.pallas import tpu as pltpu
from jax.sharding import PartitionSpec as P

W = 16
F32 = jnp.float32
BF16 = jnp.bfloat16
NN = (((1,), (0,)), ((), ()))
NT = (((1,), (1,)), ((), ()))
TN = (((0,), (0,)), ((), ()))
MESH = pl.DeviceIdType.MESH
VMEM = pl.BlockSpec(memory_space=pltpu.VMEM)
SMEM = pl.BlockSpec(memory_space=pltpu.SMEM)
HBM = pl.BlockSpec(memory_space=pltpu.HBM)


def split2(x):
    hi = x.astype(BF16)
    return hi, (x - hi.astype(F32)).astype(BF16)


def split3(x):
    hi = x.astype(BF16)
    rest = x - hi.astype(F32)
    mid = rest.astype(BF16)
    return hi, mid, (rest - mid.astype(F32)).astype(BF16)


def mm(a, b, dims):
    return lax.dot_general(a, b, dims, preferred_element_type=F32)


def dot3(a, b, dims):
    return mm(a[0], b[0], dims) + (mm(a[0], b[1], dims) + mm(a[1], b[0], dims))


def sweep_inverse(cov, begin=0, end=None):
    size = cov.shape[0]
    lane = lax.broadcasted_iota(jnp.int32, (W, size), 1)
    row = lax.broadcasted_iota(jnp.int32, (W, size), 0)
    row_small = lax.broadcasted_iota(jnp.int32, (W, 128), 0)

    def body(k, carry):
        start = pl.multiple_of(k * W, W)
        panel = cov[pl.ds(start, W), :]
        rolled = pltpu.roll(panel, size - start, 1)
        cols = [jnp.broadcast_to(rolled[:, i:i + 1], (W, 128)) for i in range(W)]
        inside = (lane >= start) & (lane < start + W)
        left = jnp.where(inside, jnp.where(lane - start == row, -1.0, 0.0), panel)
        right = left
        scale = jnp.zeros((W, 128), F32)
        for j in range(W):
            inv = 1.0 / cols[j][j:j + 1, :]
            here = row_small == j
            mult = jnp.where(here, 0.0, cols[j])
            scale = jnp.where(here, inv, scale)
            for i in range(j + 1, W):
                cols[i] = cols[i] - mult * (cols[i][j:j + 1, :] * inv)
            wide = jnp.concatenate([mult] * (size // 128), axis=1)
            wide_inv = jnp.concatenate([inv] * (size // 128), axis=1)
            right = right - wide * (right[j:j + 1, :] * wide_inv)
        right = right * jnp.concatenate([scale] * (size // 128), axis=1)
        a1, a2, a3 = split3(left)
        b1, b2, b3 = split3(right)
        lhs = jnp.concatenate([a1, a1, a2, a1, a2, a3], axis=0)
        rhs = jnp.concatenate([b1, b2, b1, b3, b2, b1], axis=0)
        change = mm(lhs, rhs, TN)
        r_ids = lax.broadcasted_iota(jnp.int32, (size, size), 0)
        c_ids = lax.broadcasted_iota(jnp.int32, (size, size), 1)
        hit = ((r_ids >= start) & (r_ids < start + W)) | ((c_ids >= start) & (c_ids < start + W))
        cov[...] = jnp.where(hit, 0.0, cov[...]) - change
        return carry

    lax.fori_loop(begin, size // W if end is None else end, body, 0)


def row_mean(x):
    return jnp.sum(x, axis=1, keepdims=True) * (1.0 / x.shape[1])


def covariance(anom2, var_ref, cov):
    size, members = anom2[0].shape
    r_ids = lax.broadcasted_iota(jnp.int32, (size, size), 0)
    c_ids = lax.broadcasted_iota(jnp.int32, (size, size), 1)
    full = dot3(anom2, anom2, NT) * (1.0 / (members - 1.0))
    cov[...] = full + jnp.where(r_ids == c_ids, jnp.broadcast_to(var_ref, (size, size)), 0.0)


def column_of(row, eye):
    return jnp.sum(jnp.where(eye, jnp.broadcast_to(row, eye.shape), 0.0), axis=1, keepdims=True)


def eye_of(count):
    return (lax.broadcasted_iota(jnp.int32, (count, count), 0)
            == lax.broadcasted_iota(jnp.int32, (count, count), 1))


def widen(values, count):
    lane = lax.broadcasted_iota(jnp.int32, (1, count), 1)
    wide = count // len(values)
    out = jnp.zeros((1, count), F32)
    for j, value in enumerate(values):
        out = jnp.where((lane >= j * wide) & (lane < (j + 1) * wide), value, out)
    return out


def taper_of(position, where, mask, local_len):
    return mask * jnp.exp(-jnp.abs(position - where) / local_len)


def my_positions(rows, count, ncols):
    first = (lax.axis_index("row") * ncols + lax.axis_index("col")) * rows
    return (first + lax.broadcasted_iota(jnp.int32, (rows, count), 0)).astype(F32)


def gain_of(anom2, obs2, neg_inv2, taper, members):
    cross = dot3(anom2, obs2, NT) * (1.0 / (members - 1.0))
    return split2(dot3(split2(taper * cross), neg_inv2, NN))


def first_batch(nrows, ncols, g_ref, x_ref, rows_ref, owner_ref, mask_ref, val_ref, var_ref,
                inv_ref, x1_ref, anom_hi, anom_lo, push_hi, push_lo, aux_ref, beside):
    rows, members = x_ref.shape
    count = rows_ref.shape[1]
    nblk = mask_ref.shape[2]
    local_len = float(rows * nrows * ncols // 4)
    g0 = g_ref[0].reshape(count, members)
    m0 = row_mean(g0)
    a0 = g0 - m0
    anom_hi[...], anom_lo[...] = split2(a0)
    covariance((anom_hi[...], anom_lo[...]), var_ref[0:1, :], inv_ref)
    beside(0)
    lane = lax.broadcasted_iota(jnp.int32, (1, count), 1)
    device = jnp.zeros((1, count), jnp.int32)
    for c in range(1, ncols):
        device = device + jnp.where(lane >= c * (count // ncols), 1, 0)
    for b in range(2):
        aux_ref[b:b + 1, :] = ((owner_ref[b] * ncols + device) * rows + rows_ref[b:b + 1, :]).astype(F32)
        aux_ref[2 + b:3 + b, :] = widen([mask_ref[b, 0, j].astype(F32) for j in range(nblk)], count)
    aux_ref[4:6, :] = val_ref[...]
    aux_ref[6:8, :] = var_ref[...]
    push_hi[...], push_lo[...] = split2(column_of(val_ref[0:1, :], eye_of(count)) - m0 - 0.5 * a0)
    steps = count // W
    cuts = [0, steps // 4, steps // 2, 13 * steps // 16, steps]
    for k in range(4):
        sweep_inverse(inv_ref, cuts[k], cuts[k + 1])
        beside(k + 1)
    x = x_ref[...]
    taper = taper_of(my_positions(rows, count, ncols), aux_ref[0:1, :], aux_ref[2:3, :], local_len)
    gain = gain_of(split2(x - row_mean(x)), (anom_hi[...], anom_lo[...]), split2(inv_ref[...]), taper, members)
    x1_ref[...] = x - dot3(gain, (push_hi[...], push_lo[...]), NN)
    beside(5)


def solo_kernel(nrows, ncols, *refs):
    first_batch(nrows, ncols, *refs, lambda stage: None)


def flip(index, bits):
    bit = 1
    while bit <= bits:
        if bits & bit:
            index = index + bit - 2 * bit * ((index // bit) % 2)
        bit *= 2
    return index


def share_kernel(nrows, ncols, x_hbm, rows_hbm, owner_hbm, mask_hbm, val_hbm, var_hbm, g_ref, note_ref,
                 inv_ref, x1_ref, anom_hi, anom_lo, push_hi, push_lo, aux_ref,
                 x_ref, rows_ref, owner_ref, mask_ref, val_ref, var_ref, load, src, core_slot, part, slots,
                 note_src, note_slots, core_s, core_r, sum_s, sum_r, line_s, line_r, plane_s, plane_r, pair_s, pair_r,
                 nsum_s, nsum_r, nline_s, nline_r):
    loads = [pltpu.make_async_copy(source, target, load.at[k]) for k, (source, target) in enumerate((
        (x_hbm, x_ref), (rows_hbm, rows_ref), (owner_hbm, owner_ref), (mask_hbm, mask_ref),
        (val_hbm, val_ref), (var_hbm, var_ref)))]
    for copy in loads:
        copy.start()
    me = lax.axis_index("row")
    col = lax.axis_index("col")
    nstate, members = x_ref.shape
    count = rows_ref.shape[1]
    per_dev = count // ncols
    q = per_dev // nrows
    half = nrows // 2
    core = me % 2
    chip = me // 2
    sibling = flip(me, 1)
    beside_x = flip(me, 2)
    beside_y = flip(me, 4)
    across = flip(me, 6)
    cut = members // 2

    barrier = pltpu.get_barrier_semaphore()
    for d in range(1, nrows):
        pl.semaphore_signal(barrier, inc=1, device_id=(flip(me, d), col), device_id_type=MESH)
    for d in range(1, ncols):
        pl.semaphore_signal(barrier, inc=1, device_id=(me, flip(col, d)), device_id_type=MESH)

    sent = []

    def put(source, target, send, recv, row, column):
        copy = pltpu.make_async_remote_copy(
            src_ref=source, dst_ref=target, send_sem=send, recv_sem=recv,
            device_id=(row, column), device_id_type=MESH)
        copy.start()
        sent.append(copy)
        return copy

    def same(ref, send, recv, row):
        return put(ref, ref, send, recv, row, col)

    for copy in loads:
        copy.wait()
    x3 = split3(x_ref[...])
    state_ids = lax.broadcasted_iota(jnp.int32, (nstate, per_dev), 0)

    def select(b):
        ids = jnp.broadcast_to(rows_ref[b:b + 1, :], (8, count))
        ids = pltpu.roll(ids, (count - col * per_dev) % count, 1)[0:1, :per_dev]
        here = jnp.full((1, per_dev), owner_ref[b], jnp.int32) == me
        ids = jnp.where(here, ids, -1)
        pick = jnp.where(ids == state_ids, 1.0, 0.0).astype(BF16)
        rows = (mm(pick, x3[0], TN) + mm(pick, x3[1], TN)) + mm(pick, x3[2], TN)
        src[b] = rows.reshape(half, 2, q, members)

    def to_core(b):
        return put(src.at[b, :, 1 - core], core_slot.at[b], core_s.at[b], core_r.at[b], sibling, col)

    def to_chips(b, copy):
        copy.wait_recv()
        part[b] = src[b, :, core] + core_slot[b]
        return [put(part.at[b, flip(chip, d)], slots.at[b, d - 1], sum_s.at[b, d - 1], sum_r.at[b, d - 1],
                    flip(me, 2 * d), col) for d in range(1, half)]

    def along_line(b, copies):
        for copy in copies:
            copy.wait_recv()
        total = part[b, chip]
        for d in range(1, half):
            total = total + slots[b, d - 1]
        g_ref[b, col, me] = total
        mine = g_ref.at[b, col, me]
        return [put(mine, mine, line_s.at[b, d - 1], line_r.at[b, d - 1], me, flip(col, d))
                for d in range(1, ncols)]

    def spread(b, d):
        slab = g_ref.at[b, flip(col, d), me]
        x_copy = same(slab, plane_s.at[b, d, 0], plane_r.at[b, d, 0], beside_x)
        y_copy = same(slab, plane_s.at[b, d, 1], plane_r.at[b, d, 1], beside_y)
        return [x_copy, y_copy], [same(slab, pair_s.at[b, d, 0], pair_r.at[b, d, 0], sibling)]

    def spread_lines(b, lines, first):
        planes, pairs = [first[0]], list(first[1])
        for d in range(1, ncols):
            lines[d - 1].wait_recv()
            more = spread(b, d)
            planes.append(more[0])
            pairs.extend(more[1])
        return planes, pairs

    def relay(b, d, planes, pairs):
        planes[d][0].wait_recv()
        slab = g_ref.at[b, flip(col, d), beside_x]
        planes[d].append(same(slab.at[:, :cut], plane_s.at[b, d, 2], plane_r.at[b, d, 2], beside_y))
        pairs.append(same(slab, pair_s.at[b, d, 1], pair_r.at[b, d, 1], sibling))
        planes[d][1].wait_recv()
        slab = g_ref.at[b, flip(col, d), beside_y]
        planes[d].append(same(slab.at[:, cut:], plane_s.at[b, d, 3], plane_r.at[b, d, 3], beside_x))
        pairs.append(same(slab, pair_s.at[b, d, 2], pair_r.at[b, d, 2], sibling))

    def relay_all(b, planes, pairs):
        for d in range(ncols):
            relay(b, d, planes, pairs)

    def finish(b, planes, pairs):
        for d in range(ncols):
            planes[d][2].wait_recv()
            planes[d][3].wait_recv()
            pairs.append(same(g_ref.at[b, flip(col, d), across], pair_s.at[b, d, 3], pair_r.at[b, d, 3], sibling))

    lane = lax.broadcasted_iota(jnp.int32, (8, 128), 1)
    note = jnp.zeros((8, 128), F32)
    for j in range(mask_ref.shape[2]):
        note = jnp.where(lane == j, mask_ref[0, 0, j].astype(F32), note)
    here = jnp.full((8, 128), owner_ref[1], jnp.int32) == me
    note_src[...] = jnp.where(here, note, 0.0)
    select(0)
    pl.semaphore_wait(barrier, nrows + ncols - 2)
    core0 = to_core(0)
    select(1)
    sums0 = to_chips(0, core0)
    core1 = to_core(1)
    lines0 = along_line(0, sums0)
    first0 = spread(0, 0)
    notes = [put(note_src, note_slots.at[d - 1], nsum_s.at[d - 1], nsum_r.at[d - 1], flip(me, d), col)
             for d in range(1, nrows)]
    planes0, pairs0 = spread_lines(0, lines0, first0)
    relay_all(0, planes0, pairs0)
    sums1 = to_chips(1, core1)
    finish(0, planes0, pairs0)
    total = note_src[...]
    for d in range(1, nrows):
        notes[d - 1].wait_recv()
        total = total + note_slots[d - 1]
    note_ref[col] = total
    note_lines = [put(note_ref.at[col], note_ref.at[col], nline_s.at[d - 1], nline_r.at[d - 1], me, flip(col, d))
                  for d in range(1, ncols)]
    for copy in pairs0:
        copy.wait_recv()
    later = []

    def beside(stage):
        if stage == 0:
            lines1 = along_line(1, sums1)
            later.extend([lines1, spread(1, 0)])
        elif stage == 1:
            later[:] = spread_lines(1, *later)
        elif stage == 2:
            relay_all(1, *later)
        elif stage == 3:
            finish(1, *later)
        elif stage == 5:
            for copy in later[1] + note_lines:
                copy.wait_recv()

    first_batch(nrows, ncols, g_ref, x_ref, rows_ref, owner_ref, mask_ref, val_ref, var_ref,
                inv_ref, x1_ref, anom_hi, anom_lo, push_hi, push_lo, aux_ref, beside)
    for copy in sent:
        copy.wait_send()


def second_kernel(nrows, ncols, nblk, g_ref, note_ref, inv_ref, x1_ref, anom_hi, anom_lo, push_hi, push_lo, aux_ref,
                  out_ref, g1, cov):
    rows, members = x1_ref.shape
    count = inv_ref.shape[0]
    local_len = float(rows * nrows * ncols // 4)
    eye = eye_of(count)
    mask_g = jnp.concatenate(
        [jnp.broadcast_to(widen([note_ref[c, 0:1, j:j + 1] for j in range(nblk)], count), (count // ncols, count))
         for c in range(ncols)], axis=0)
    taper = taper_of(column_of(aux_ref[1:2, :], eye), aux_ref[0:1, :], mask_g, local_len)
    g = g_ref[1].reshape(count, members)
    gain = gain_of(split2(g - row_mean(g)), (anom_hi[...], anom_lo[...]), split2(inv_ref[...]), taper, members)
    g1[...] = g - dot3(gain, (push_hi[...], push_lo[...]), NN)
    g = g1[...]
    m1 = row_mean(g)
    a1 = g - m1
    a12 = split2(a1)
    covariance(a12, aux_ref[7:8, :], cov)
    sweep_inverse(cov)
    push = split2(column_of(aux_ref[5:6, :], eye) - m1 - 0.5 * a1)
    x = x1_ref[...]
    taper = taper_of(my_positions(rows, count, ncols), aux_ref[1:2, :], aux_ref[3:4, :], local_len)
    gain = gain_of(split2(x - row_mean(x)), a12, split2(cov[...]), taper, members)
    out_ref[...] = x - dot3(gain, push, NN)


def shared_by_collectives(ensemble, obs_rows, owner, taper_mask, ncols):
    rows, members = ensemble.shape
    batches, count = obs_rows.shape
    per_dev = count // ncols
    nblk = taper_mask.shape[2]
    my_row = lax.axis_index("row")
    mine = lax.dynamic_slice_in_dim(obs_rows, lax.axis_index("col") * per_dev, per_dev, axis=1)
    row_ids = jnp.arange(rows, dtype=jnp.int32)
    shared = []
    for batch in range(batches):
        here = owner[batch] == my_row
        picker = ((mine[batch][:, None] == row_ids[None, :]) & here).astype(F32)
        part = jnp.dot(picker, ensemble, precision=lax.Precision.HIGHEST)
        shared.append(lax.all_gather(lax.psum(part, "row"), "col", axis=0).reshape(count, members))
    note = jnp.where(owner[1] == my_row, taper_mask[0, 0].astype(F32), 0.0)
    note = jnp.pad(jnp.broadcast_to(note[None, :], (8, nblk)), ((0, 0), (0, 128 - nblk)))
    note = lax.all_gather(lax.psum(note, "row"), "col", axis=0)
    return jnp.stack(shared), note


def on_device(nrows, ncols, ensemble, obs_rows, owner, obs_value, obs_var, taper_mask):
    rows, members = ensemble.shape
    batches, count = obs_rows.shape
    per_dev = count // ncols
    half_shape = jax.ShapeDtypeStruct((count, members), BF16)
    kept = (
        jax.ShapeDtypeStruct((count, count), F32),
        jax.ShapeDtypeStruct((rows, members), F32),
        half_shape, half_shape, half_shape, half_shape,
        jax.ShapeDtypeStruct((8, count), F32),
    )
    limit = 40 * 2**20
    if nrows == 8 and ncols & (ncols - 1) == 0 and per_dev % (8 * nrows) == 0:
        q = per_dev // nrows
        half = nrows // 2
        dma = pltpu.SemaphoreType.DMA
        shared, note, *held = pl.pallas_call(
            functools.partial(share_kernel, nrows, ncols),
            out_shape=(
                jax.ShapeDtypeStruct((batches, ncols, nrows, q, members), F32),
                jax.ShapeDtypeStruct((ncols, 8, 128), F32),
            ) + kept,
            in_specs=[HBM] * 6,
            out_specs=(VMEM,) * 9,
            scratch_shapes=[
                pltpu.VMEM(ensemble.shape, F32),
                pltpu.VMEM(obs_rows.shape, jnp.int32),
                pltpu.SMEM(owner.shape, jnp.int32),
                pltpu.SMEM(taper_mask.shape, jnp.int32),
                pltpu.VMEM(obs_value.shape, F32),
                pltpu.VMEM(obs_var.shape, F32),
                dma((6,)),
                pltpu.VMEM((batches, half, 2, q, members), F32),
                pltpu.VMEM((batches, half, q, members), F32),
                pltpu.VMEM((batches, half, q, members), F32),
                pltpu.VMEM((batches, half - 1, q, members), F32),
                pltpu.VMEM((8, 128), F32),
                pltpu.VMEM((nrows - 1, 8, 128), F32),
            ] + [dma((batches,))] * 2 + [dma((batches, half - 1))] * 2 + [dma((batches, ncols - 1))] * 2
            + [dma((batches, ncols, 4))] * 4 + [dma((nrows - 1,))] * 2 + [dma((ncols - 1,))] * 2,
            compiler_params=pltpu.CompilerParams(
                vmem_limit_bytes=limit, collective_id=0, has_side_effects=True),
        )(*[pltpu.with_memory_space_constraint(arg, pltpu.HBM)
            for arg in (ensemble, obs_rows, owner, taper_mask, obs_value, obs_var)])
    else:
        shared, note = shared_by_collectives(ensemble, obs_rows, owner, taper_mask, ncols)
        held = pl.pallas_call(
            functools.partial(solo_kernel, nrows, ncols),
            out_shape=kept,
            in_specs=[VMEM] * 3 + [SMEM] * 2 + [VMEM] * 2,
            out_specs=(VMEM,) * 7,
            compiler_params=pltpu.CompilerParams(vmem_limit_bytes=limit),
        )(shared, ensemble, obs_rows, owner, taper_mask, obs_value, obs_var)
    return pl.pallas_call(
        functools.partial(second_kernel, nrows, ncols, taper_mask.shape[2]),
        out_shape=jax.ShapeDtypeStruct((rows, members), F32),
        in_specs=[VMEM] * 9,
        out_specs=VMEM,
        scratch_shapes=[pltpu.VMEM((count, members), F32), pltpu.VMEM((count, count), F32)],
        compiler_params=pltpu.CompilerParams(vmem_limit_bytes=limit),
    )(shared, note, *held)


def solution(mesh):
    in_specs = (P(("row", "col"), None), P(), P(), P(), P(), P(None, ("row", "col"), None))
    out_specs = P(("row", "col"), None)
    return jax.shard_map(
        functools.partial(on_device, mesh.shape["row"], mesh.shape["col"]),
        mesh=mesh, in_specs=in_specs, out_specs=out_specs, check_vma=False
    )
```

```python
import functools

import jax
import jax.numpy as jnp
from jax import lax
from jax.experimental import pallas as pl
from jax.experimental.pallas import tpu as pltpu
from jax.sharding import PartitionSpec as P

W = 16
F32 = jnp.float32
BF16 = jnp.bfloat16
NN = (((1,), (0,)), ((), ()))
NT = (((1,), (1,)), ((), ()))
TN = (((0,), (0,)), ((), ()))
MESH = pl.DeviceIdType.MESH
VMEM = pl.BlockSpec(memory_space=pltpu.VMEM)
SMEM = pl.BlockSpec(memory_space=pltpu.SMEM)
HBM = pl.BlockSpec(memory_space=pltpu.HBM)


def split2(x):
    hi = x.astype(BF16)
    return hi, (x - hi.astype(F32)).astype(BF16)


def split3(x):
    hi = x.astype(BF16)
    rest = x - hi.astype(F32)
    mid = rest.astype(BF16)
    return hi, mid, (rest - mid.astype(F32)).astype(BF16)


def mm(a, b, dims):
    return lax.dot_general(a, b, dims, preferred_element_type=F32)


def dot3(a, b, dims):
    return mm(a[0], b[0], dims) + (mm(a[0], b[1], dims) + mm(a[1], b[0], dims))


def eliminate(cols, right):
    size = right.shape[1]
    row = lax.broadcasted_iota(jnp.int32, (W, 128), 0)
    same = jnp.zeros((W, 128), F32)
    other = jnp.zeros((W, 128), F32)
    widen_lanes = lambda v: jnp.concatenate([v] * (size // 128), axis=1)
    for j in range(0, W, 2):
        a, b, d = cols[j][j:j + 1, :], cols[j + 1][j:j + 1, :], cols[j + 1][j + 1:j + 2, :]
        det = a * d - b * b
        r = pl.reciprocal(det, approx=True)
        r = r * (2.0 - det * r)
        r = r * (2.0 - det * r)
        ar, br, dr = a * r, b * r, d * r
        pair = (row == j) | (row == j + 1)
        m1 = jnp.where(pair, 0.0, cols[j])
        m2 = jnp.where(pair, 0.0, cols[j + 1])
        same = jnp.where(row == j, dr, jnp.where(row == j + 1, ar, same))
        other = jnp.where(pair, br, other)
        for i in range(j + 2, W):
            x, y = cols[i][j:j + 1, :], cols[i][j + 1:j + 2, :]
            cols[i] = cols[i] - m1 * (dr * x - br * y) - m2 * (ar * y - br * x)
        x, y = right[j:j + 1, :], right[j + 1:j + 2, :]
        arw, brw, drw = widen_lanes(ar), widen_lanes(br), widen_lanes(dr)
        right = right - widen_lanes(m1) * (drw * x - brw * y) - widen_lanes(m2) * (arw * y - brw * x)
    even = lax.broadcasted_iota(jnp.int32, (W, size), 0) % 2 == 0
    swapped = jnp.where(even, pltpu.roll(right, W - 1, 0), pltpu.roll(right, 1, 0))
    return right * widen_lanes(same) - swapped * widen_lanes(other)


def six_terms(left, right):
    a1, a2, a3 = split3(left)
    b1, b2, b3 = split3(right)
    return (jnp.concatenate([a1, a1, a2, a1, a2, a3], axis=0), jnp.concatenate([b1, b2, b1, b3, b2, b1], axis=0))


def sweep_apply(cov, lhs, rhs, start):
    lane = lax.broadcasted_iota(jnp.int32, (1, cov.shape[1]), 1)
    inside = (lane >= start) & (lane < start + W)
    cov[...] = jnp.where(inside, 0.0, cov[...]) - mm(lhs[...], rhs[...], TN)


def sweep_begin(cov, lhs, rhs):
    lhs[...] = jnp.zeros(lhs.shape, BF16)
    rhs[...] = jnp.zeros(rhs.shape, BF16)
    return cov[0:W, :]


def sweep_steps(cov, lhs, rhs, panel, begin, end):
    size = cov.shape[0]
    lane = lax.broadcasted_iota(jnp.int32, (W, size), 1)
    row = lax.broadcasted_iota(jnp.int32, (W, size), 0)

    def body(k, panel):
        start = pl.multiple_of(k * W, W)
        sweep_apply(cov, lhs, rhs, start - W)
        cov[pl.ds(start, W), :] = jnp.zeros((W, size), F32)
        rolled = pltpu.roll(panel, size - start, 1)
        cols = [jnp.broadcast_to(rolled[:, i:i + 1], (W, 128)) for i in range(W)]
        inside = (lane >= start) & (lane < start + W)
        left = jnp.where(inside, jnp.where(lane - start == row, -1.0, 0.0), panel)
        right = eliminate(cols, left)
        after = ((k + 1) % (size // W)) * W
        lhs[...], rhs[...] = six_terms(left, right)
        ahead, _ = six_terms(pltpu.roll(left, size - after, 1)[:, :128], left)
        coming = jnp.where(inside, 0.0, cov[pl.ds(pl.multiple_of(after, W), W), :])
        return coming - mm(ahead, rhs[...], TN)[:W, :]

    return lax.fori_loop(begin, end, body, panel)


def sweep_end(cov, lhs, rhs):
    sweep_apply(cov, lhs, rhs, cov.shape[0] - W)


def row_mean(x):
    return jnp.sum(x, axis=1, keepdims=True) * (1.0 / x.shape[1])


def covariance(anom2, var_ref, cov):
    size, members = anom2[0].shape
    r_ids = lax.broadcasted_iota(jnp.int32, (size, size), 0)
    c_ids = lax.broadcasted_iota(jnp.int32, (size, size), 1)
    full = dot3(anom2, anom2, NT) * (1.0 / (members - 1.0))
    cov[...] = full + jnp.where(r_ids == c_ids, jnp.broadcast_to(var_ref, (size, size)), 0.0)


def column_of(row, eye):
    return jnp.sum(jnp.where(eye, jnp.broadcast_to(row, eye.shape), 0.0), axis=1, keepdims=True)


def eye_of(count):
    return (lax.broadcasted_iota(jnp.int32, (count, count), 0)
            == lax.broadcasted_iota(jnp.int32, (count, count), 1))


def widen(values, count):
    lane = lax.broadcasted_iota(jnp.int32, (1, count), 1)
    wide = count // len(values)
    out = jnp.zeros((1, count), F32)
    for j, value in enumerate(values):
        out = jnp.where((lane >= j * wide) & (lane < (j + 1) * wide), value, out)
    return out


def taper_of(position, where, mask, local_len):
    return mask * jnp.exp(-jnp.abs(position - where) / local_len)


def my_positions(rows, count, ncols):
    first = (lax.axis_index("row") * ncols + lax.axis_index("col")) * rows
    return (first + lax.broadcasted_iota(jnp.int32, (rows, count), 0)).astype(F32)


def gain_of(anom2, obs2, neg_inv2, taper, members):
    cross = dot3(anom2, obs2, NT) * (1.0 / (members - 1.0))
    return split2(dot3(split2(taper * cross), neg_inv2, NN))


def first_batch(nrows, ncols, g_ref, x_ref, rows_ref, owner_ref, mask_ref, val_ref, var_ref,
                inv_ref, x1_ref, anom_hi, anom_lo, push_hi, push_lo, aux_ref, lhs, rhs, beside):
    rows, members = x_ref.shape
    count = rows_ref.shape[1]
    nblk = mask_ref.shape[2]
    local_len = float(rows * nrows * ncols // 4)
    g0 = g_ref[0].reshape(count, members)
    m0 = row_mean(g0)
    a0 = g0 - m0
    anom_hi[...], anom_lo[...] = split2(a0)
    covariance((anom_hi[...], anom_lo[...]), var_ref[0:1, :], inv_ref)
    beside(0)
    lane = lax.broadcasted_iota(jnp.int32, (1, count), 1)
    device = jnp.zeros((1, count), jnp.int32)
    for c in range(1, ncols):
        device = device + jnp.where(lane >= c * (count // ncols), 1, 0)
    for b in range(2):
        aux_ref[b:b + 1, :] = ((owner_ref[b] * ncols + device) * rows + rows_ref[b:b + 1, :]).astype(F32)
        aux_ref[2 + b:3 + b, :] = widen([mask_ref[b, 0, j].astype(F32) for j in range(nblk)], count)
    aux_ref[4:6, :] = val_ref[...]
    aux_ref[6:8, :] = var_ref[...]
    push_hi[...], push_lo[...] = split2(column_of(val_ref[0:1, :], eye_of(count)) - m0 - 0.5 * a0)
    steps = count // W
    cuts = [0, steps // 4, steps // 2, 13 * steps // 16, steps]
    panel = sweep_begin(inv_ref, lhs, rhs)
    for k in range(4):
        panel = sweep_steps(inv_ref, lhs, rhs, panel, cuts[k], cuts[k + 1])
        beside(k + 1)
    sweep_end(inv_ref, lhs, rhs)
    x = x_ref[...]
    taper = taper_of(my_positions(rows, count, ncols), aux_ref[0:1, :], aux_ref[2:3, :], local_len)
    gain = gain_of(split2(x - row_mean(x)), (anom_hi[...], anom_lo[...]), split2(inv_ref[...]), taper, members)
    x1_ref[...] = x - dot3(gain, (push_hi[...], push_lo[...]), NN)
    beside(5)


def solo_kernel(nrows, ncols, *refs):
    first_batch(nrows, ncols, *refs, lambda stage: None)


def flip(index, bits):
    bit = 1
    while bit <= bits:
        if bits & bit:
            index = index + bit - 2 * bit * ((index // bit) % 2)
        bit *= 2
    return index


def share_kernel(nrows, ncols, x_hbm, rows_hbm, owner_hbm, mask_hbm, val_hbm, var_hbm, g_ref, note_ref,
                 inv_ref, x1_ref, anom_hi, anom_lo, push_hi, push_lo, aux_ref,
                 lhs, rhs, x_ref, rows_ref, owner_ref, mask_ref, val_ref, var_ref, load, src, core_slot, part, slots,
                 note_src, note_slots, core_s, core_r, sum_s, sum_r, line_s, line_r, plane_s, plane_r, pair_s, pair_r,
                 nsum_s, nsum_r, nline_s, nline_r):
    loads = [pltpu.make_async_copy(source, target, load.at[k]) for k, (source, target) in enumerate((
        (x_hbm, x_ref), (rows_hbm, rows_ref), (owner_hbm, owner_ref), (mask_hbm, mask_ref),
        (val_hbm, val_ref), (var_hbm, var_ref)))]
    for copy in loads:
        copy.start()
    me = lax.axis_index("row")
    col = lax.axis_index("col")
    nstate, members = x_ref.shape
    count = rows_ref.shape[1]
    per_dev = count // ncols
    q = per_dev // nrows
    half = nrows // 2
    core = me % 2
    chip = me // 2
    sibling = flip(me, 1)
    beside_x = flip(me, 2)
    beside_y = flip(me, 4)
    across = flip(me, 6)
    cut = members // 2

    barrier = pltpu.get_barrier_semaphore()
    for d in range(1, nrows):
        pl.semaphore_signal(barrier, inc=1, device_id=(flip(me, d), col), device_id_type=MESH)
    for d in range(1, ncols):
        pl.semaphore_signal(barrier, inc=1, device_id=(me, flip(col, d)), device_id_type=MESH)

    sent = []

    def put(source, target, send, recv, row, column):
        copy = pltpu.make_async_remote_copy(
            src_ref=source, dst_ref=target, send_sem=send, recv_sem=recv,
            device_id=(row, column), device_id_type=MESH)
        copy.start()
        sent.append(copy)
        return copy

    def same(ref, send, recv, row):
        return put(ref, ref, send, recv, row, col)

    for copy in loads:
        copy.wait()
    x3 = split3(x_ref[...])
    state_ids = lax.broadcasted_iota(jnp.int32, (nstate, per_dev), 0)

    def select(b):
        ids = jnp.broadcast_to(rows_ref[b:b + 1, :], (8, count))
        ids = pltpu.roll(ids, (count - col * per_dev) % count, 1)[0:1, :per_dev]
        here = jnp.full((1, per_dev), owner_ref[b], jnp.int32) == me
        ids = jnp.where(here, ids, -1)
        pick = jnp.where(ids == state_ids, 1.0, 0.0).astype(BF16)
        rows = (mm(pick, x3[0], TN) + mm(pick, x3[1], TN)) + mm(pick, x3[2], TN)
        src[b] = rows.reshape(half, 2, q, members)

    def to_core(b):
        return put(src.at[b, :, 1 - core], core_slot.at[b], core_s.at[b], core_r.at[b], sibling, col)

    def to_chips(b, copy):
        copy.wait_recv()
        part[b] = src[b, :, core] + core_slot[b]
        return [put(part.at[b, flip(chip, d)], slots.at[b, d - 1], sum_s.at[b, d - 1], sum_r.at[b, d - 1],
                    flip(me, 2 * d), col) for d in range(1, half)]

    def along_line(b, copies):
        for copy in copies:
            copy.wait_recv()
        total = part[b, chip]
        for d in range(1, half):
            total = total + slots[b, d - 1]
        g_ref[b, col, me] = total
        mine = g_ref.at[b, col, me]
        return [put(mine, mine, line_s.at[b, d - 1], line_r.at[b, d - 1], me, flip(col, d))
                for d in range(1, ncols)]

    def spread(b, d):
        slab = g_ref.at[b, flip(col, d), me]
        x_copy = same(slab, plane_s.at[b, d, 0], plane_r.at[b, d, 0], beside_x)
        y_copy = same(slab, plane_s.at[b, d, 1], plane_r.at[b, d, 1], beside_y)
        return [x_copy, y_copy], [same(slab, pair_s.at[b, d, 0], pair_r.at[b, d, 0], sibling)]

    def spread_lines(b, lines, first):
        planes, pairs = [first[0]], list(first[1])
        for d in range(1, ncols):
            lines[d - 1].wait_recv()
            more = spread(b, d)
            planes.append(more[0])
            pairs.extend(more[1])
        return planes, pairs

    def relay(b, d, planes, pairs):
        planes[d][0].wait_recv()
        slab = g_ref.at[b, flip(col, d), beside_x]
        planes[d].append(same(slab.at[:, :cut], plane_s.at[b, d, 2], plane_r.at[b, d, 2], beside_y))
        pairs.append(same(slab, pair_s.at[b, d, 1], pair_r.at[b, d, 1], sibling))
        planes[d][1].wait_recv()
        slab = g_ref.at[b, flip(col, d), beside_y]
        planes[d].append(same(slab.at[:, cut:], plane_s.at[b, d, 3], plane_r.at[b, d, 3], beside_x))
        pairs.append(same(slab, pair_s.at[b, d, 2], pair_r.at[b, d, 2], sibling))

    def relay_all(b, planes, pairs):
        for d in range(ncols):
            relay(b, d, planes, pairs)

    def finish(b, planes, pairs):
        for d in range(ncols):
            planes[d][2].wait_recv()
            planes[d][3].wait_recv()
            pairs.append(same(g_ref.at[b, flip(col, d), across], pair_s.at[b, d, 3], pair_r.at[b, d, 3], sibling))

    lane = lax.broadcasted_iota(jnp.int32, (8, 128), 1)
    note = jnp.zeros((8, 128), F32)
    for j in range(mask_ref.shape[2]):
        note = jnp.where(lane == j, mask_ref[0, 0, j].astype(F32), note)
    here = jnp.full((8, 128), owner_ref[1], jnp.int32) == me
    note_src[...] = jnp.where(here, note, 0.0)
    select(0)
    pl.semaphore_wait(barrier, nrows + ncols - 2)
    core0 = to_core(0)
    select(1)
    sums0 = to_chips(0, core0)
    core1 = to_core(1)
    lines0 = along_line(0, sums0)
    first0 = spread(0, 0)
    notes = [put(note_src, note_slots.at[d - 1], nsum_s.at[d - 1], nsum_r.at[d - 1], flip(me, d), col)
             for d in range(1, nrows)]
    planes0, pairs0 = spread_lines(0, lines0, first0)
    relay_all(0, planes0, pairs0)
    sums1 = to_chips(1, core1)
    finish(0, planes0, pairs0)
    total = note_src[...]
    for d in range(1, nrows):
        notes[d - 1].wait_recv()
        total = total + note_slots[d - 1]
    note_ref[col] = total
    note_lines = [put(note_ref.at[col], note_ref.at[col], nline_s.at[d - 1], nline_r.at[d - 1], me, flip(col, d))
                  for d in range(1, ncols)]
    for copy in pairs0:
        copy.wait_recv()
    later = []

    def beside(stage):
        if stage == 0:
            lines1 = along_line(1, sums1)
            later.extend([lines1, spread(1, 0)])
        elif stage == 1:
            later[:] = spread_lines(1, *later)
        elif stage == 2:
            relay_all(1, *later)
        elif stage == 3:
            finish(1, *later)
        elif stage == 5:
            for copy in later[1] + note_lines:
                copy.wait_recv()

    first_batch(nrows, ncols, g_ref, x_ref, rows_ref, owner_ref, mask_ref, val_ref, var_ref,
                inv_ref, x1_ref, anom_hi, anom_lo, push_hi, push_lo, aux_ref, lhs, rhs, beside)
    for copy in sent:
        copy.wait_send()


def second_kernel(nrows, ncols, nblk, g_ref, note_ref, inv_ref, x1_ref, anom_hi, anom_lo, push_hi, push_lo, aux_ref,
                  out_ref, g1, cov, lhs, rhs):
    rows, members = x1_ref.shape
    count = inv_ref.shape[0]
    local_len = float(rows * nrows * ncols // 4)
    eye = eye_of(count)
    mask_g = jnp.concatenate(
        [jnp.broadcast_to(widen([note_ref[c, 0:1, j:j + 1] for j in range(nblk)], count), (count // ncols, count))
         for c in range(ncols)], axis=0)
    taper = taper_of(column_of(aux_ref[1:2, :], eye), aux_ref[0:1, :], mask_g, local_len)
    g = g_ref[1].reshape(count, members)
    gain = gain_of(split2(g - row_mean(g)), (anom_hi[...], anom_lo[...]), split2(inv_ref[...]), taper, members)
    g1[...] = g - dot3(gain, (push_hi[...], push_lo[...]), NN)
    g = g1[...]
    m1 = row_mean(g)
    a1 = g - m1
    a12 = split2(a1)
    covariance(a12, aux_ref[7:8, :], cov)
    panel = sweep_begin(cov, lhs, rhs)
    sweep_steps(cov, lhs, rhs, panel, 0, count // W)
    sweep_end(cov, lhs, rhs)
    push = split2(column_of(aux_ref[5:6, :], eye) - m1 - 0.5 * a1)
    x = x1_ref[...]
    taper = taper_of(my_positions(rows, count, ncols), aux_ref[1:2, :], aux_ref[3:4, :], local_len)
    gain = gain_of(split2(x - row_mean(x)), a12, split2(cov[...]), taper, members)
    out_ref[...] = x - dot3(gain, push, NN)


def shared_by_collectives(ensemble, obs_rows, owner, taper_mask, ncols):
    rows, members = ensemble.shape
    batches, count = obs_rows.shape
    per_dev = count // ncols
    nblk = taper_mask.shape[2]
    my_row = lax.axis_index("row")
    mine = lax.dynamic_slice_in_dim(obs_rows, lax.axis_index("col") * per_dev, per_dev, axis=1)
    row_ids = jnp.arange(rows, dtype=jnp.int32)
    shared = []
    for batch in range(batches):
        here = owner[batch] == my_row
        picker = ((mine[batch][:, None] == row_ids[None, :]) & here).astype(F32)
        part = jnp.dot(picker, ensemble, precision=lax.Precision.HIGHEST)
        shared.append(lax.all_gather(lax.psum(part, "row"), "col", axis=0).reshape(count, members))
    note = jnp.where(owner[1] == my_row, taper_mask[0, 0].astype(F32), 0.0)
    note = jnp.pad(jnp.broadcast_to(note[None, :], (8, nblk)), ((0, 0), (0, 128 - nblk)))
    note = lax.all_gather(lax.psum(note, "row"), "col", axis=0)
    return jnp.stack(shared), note


def on_device(nrows, ncols, ensemble, obs_rows, owner, obs_value, obs_var, taper_mask):
    rows, members = ensemble.shape
    batches, count = obs_rows.shape
    per_dev = count // ncols
    half_shape = jax.ShapeDtypeStruct((count, members), BF16)
    kept = (
        jax.ShapeDtypeStruct((count, count), F32),
        jax.ShapeDtypeStruct((rows, members), F32),
        half_shape, half_shape, half_shape, half_shape,
        jax.ShapeDtypeStruct((8, count), F32),
    )
    limit = 40 * 2**20
    terms = [pltpu.VMEM((6 * W, count), BF16)] * 2
    if nrows == 8 and ncols & (ncols - 1) == 0 and per_dev % (8 * nrows) == 0:
        q = per_dev // nrows
        half = nrows // 2
        dma = pltpu.SemaphoreType.DMA
        shared, note, *held = pl.pallas_call(
            functools.partial(share_kernel, nrows, ncols),
            out_shape=(
                jax.ShapeDtypeStruct((batches, ncols, nrows, q, members), F32),
                jax.ShapeDtypeStruct((ncols, 8, 128), F32),
            ) + kept,
            in_specs=[HBM] * 6,
            out_specs=(VMEM,) * 9,
            scratch_shapes=terms + [
                pltpu.VMEM(ensemble.shape, F32),
                pltpu.VMEM(obs_rows.shape, jnp.int32),
                pltpu.SMEM(owner.shape, jnp.int32),
                pltpu.SMEM(taper_mask.shape, jnp.int32),
                pltpu.VMEM(obs_value.shape, F32),
                pltpu.VMEM(obs_var.shape, F32),
                dma((6,)),
                pltpu.VMEM((batches, half, 2, q, members), F32),
                pltpu.VMEM((batches, half, q, members), F32),
                pltpu.VMEM((batches, half, q, members), F32),
                pltpu.VMEM((batches, half - 1, q, members), F32),
                pltpu.VMEM((8, 128), F32),
                pltpu.VMEM((nrows - 1, 8, 128), F32),
            ] + [dma((batches,))] * 2 + [dma((batches, half - 1))] * 2 + [dma((batches, ncols - 1))] * 2
            + [dma((batches, ncols, 4))] * 4 + [dma((nrows - 1,))] * 2 + [dma((ncols - 1,))] * 2,
            compiler_params=pltpu.CompilerParams(
                vmem_limit_bytes=limit, collective_id=0, has_side_effects=True),
        )(*[pltpu.with_memory_space_constraint(arg, pltpu.HBM)
            for arg in (ensemble, obs_rows, owner, taper_mask, obs_value, obs_var)])
    else:
        shared, note = shared_by_collectives(ensemble, obs_rows, owner, taper_mask, ncols)
        held = pl.pallas_call(
            functools.partial(solo_kernel, nrows, ncols),
            out_shape=kept,
            in_specs=[VMEM] * 3 + [SMEM] * 2 + [VMEM] * 2,
            out_specs=(VMEM,) * 7,
            scratch_shapes=terms,
            compiler_params=pltpu.CompilerParams(vmem_limit_bytes=limit),
        )(shared, ensemble, obs_rows, owner, taper_mask, obs_value, obs_var)
    return pl.pallas_call(
        functools.partial(second_kernel, nrows, ncols, taper_mask.shape[2]),
        out_shape=jax.ShapeDtypeStruct((rows, members), F32),
        in_specs=[VMEM] * 9,
        out_specs=VMEM,
        scratch_shapes=[pltpu.VMEM((count, members), F32), pltpu.VMEM((count, count), F32)] + terms,
        compiler_params=pltpu.CompilerParams(vmem_limit_bytes=limit),
    )(shared, note, *held)


def solution(mesh):
    in_specs = (P(("row", "col"), None), P(), P(), P(), P(), P(None, ("row", "col"), None))
    out_specs = P(("row", "col"), None)
    return jax.shard_map(
        functools.partial(on_device, mesh.shape["row"], mesh.shape["col"]),
        mesh=mesh, in_specs=in_specs, out_specs=out_specs, check_vma=False
    )
```

```python
import functools

import jax
import jax.numpy as jnp
from jax import lax
from jax.experimental import pallas as pl
from jax.experimental.pallas import tpu as pltpu
from jax.sharding import PartitionSpec as P

W = 16
F32 = jnp.float32
BF16 = jnp.bfloat16
NN = (((1,), (0,)), ((), ()))
NT = (((1,), (1,)), ((), ()))
TN = (((0,), (0,)), ((), ()))
MESH = pl.DeviceIdType.MESH
VMEM = pl.BlockSpec(memory_space=pltpu.VMEM)
SMEM = pl.BlockSpec(memory_space=pltpu.SMEM)
HBM = pl.BlockSpec(memory_space=pltpu.HBM)


def split2(x):
    hi = x.astype(BF16)
    return hi, (x - hi.astype(F32)).astype(BF16)


def split3(x):
    hi = x.astype(BF16)
    rest = x - hi.astype(F32)
    mid = rest.astype(BF16)
    return hi, mid, (rest - mid.astype(F32)).astype(BF16)


def mm(a, b, dims):
    return lax.dot_general(a, b, dims, preferred_element_type=F32)


def dot3(a, b, dims):
    return mm(a[0], b[0], dims) + (mm(a[0], b[1], dims) + mm(a[1], b[0], dims))


def eliminate(panel, right):
    size = right.shape[1]
    tiles = range(W // 8)
    row = lax.broadcasted_iota(jnp.int32, (8, 128), 0)
    cols = [[jnp.broadcast_to(panel[8 * t:8 * t + 8, i:i + 1], (8, 128)) for t in tiles] for i in range(W)]
    right = [[right[8 * t:8 * t + 8, h * 128:h * 128 + 128] for t in tiles] for h in range(size // 128)]
    same = [jnp.zeros((8, 128), F32) for t in tiles]
    other = [jnp.zeros((8, 128), F32) for t in tiles]
    for j in range(0, W, 2):
        home, at = j // 8, j % 8
        take = lambda v, k: jnp.broadcast_to(v[home][k:k + 1, :], (8, 128))
        a, b, d = take(cols[j], at), take(cols[j + 1], at), take(cols[j + 1], at + 1)
        det = a * d - b * b
        r = pl.reciprocal(det, approx=True)
        r = r * (2.0 - det * r)
        r = r * (2.0 - det * r)
        ar, br, dr = a * r, b * r, d * r
        pair = (row == at) | (row == at + 1)
        m1, m2 = list(cols[j]), list(cols[j + 1])
        m1[home] = jnp.where(pair, 0.0, m1[home])
        m2[home] = jnp.where(pair, 0.0, m2[home])
        same[home] = jnp.where(row == at, dr, jnp.where(row == at + 1, ar, same[home]))
        other[home] = jnp.where(pair, br, other[home])

        def reduced(v):
            x, y = take(v, at), take(v, at + 1)
            first, second = dr * x - br * y, ar * y - br * x
            return [v[t] - m1[t] * first - m2[t] * second for t in tiles]

        for i in range(j + 2, W):
            cols[i] = reduced(cols[i])
        right = [reduced(v) for v in right]
    even = row % 2 == 0
    done = [[v[t] * same[t] - jnp.where(even, pltpu.roll(v[t], 7, 0), pltpu.roll(v[t], 1, 0)) * other[t] for t in tiles]
            for v in right]
    return jnp.concatenate([jnp.concatenate(v, axis=0) for v in done], axis=1)


def six_terms(left, right):
    a1, a2, a3 = split3(left)
    b1, b2, b3 = split3(right)
    return (jnp.concatenate([a1, a1, a2, a1, a2, a3], axis=0), jnp.concatenate([b1, b2, b1, b3, b2, b1], axis=0))


def sweep_apply(cov, lhs, rhs, start):
    lane = lax.broadcasted_iota(jnp.int32, (1, cov.shape[1]), 1)
    inside = (lane >= start) & (lane < start + W)
    cov[...] = jnp.where(inside, 0.0, cov[...]) - mm(lhs[...], rhs[...], TN)


def sweep_begin(cov, lhs, rhs):
    lhs[...] = jnp.zeros(lhs.shape, BF16)
    rhs[...] = jnp.zeros(rhs.shape, BF16)
    return cov[0:W, :]


def sweep_steps(cov, lhs, rhs, panel, begin, end):
    size = cov.shape[0]
    lane = lax.broadcasted_iota(jnp.int32, (W, size), 1)
    row = lax.broadcasted_iota(jnp.int32, (W, size), 0)

    def body(k, panel):
        start = pl.multiple_of(k * W, W)
        sweep_apply(cov, lhs, rhs, start - W)
        cov[pl.ds(start, W), :] = jnp.zeros((W, size), F32)
        rolled = pltpu.roll(panel, size - start, 1)
        inside = (lane >= start) & (lane < start + W)
        left = jnp.where(inside, jnp.where(lane - start == row, -1.0, 0.0), panel)
        right = eliminate(rolled, left)
        after = ((k + 1) % (size // W)) * W
        lhs[...], rhs[...] = six_terms(left, right)
        ahead, _ = six_terms(pltpu.roll(left, size - after, 1)[:, :128], left)
        coming = jnp.where(inside, 0.0, cov[pl.ds(pl.multiple_of(after, W), W), :])
        return coming - mm(ahead, rhs[...], TN)[:W, :]

    return lax.fori_loop(begin, end, body, panel)


def sweep_end(cov, lhs, rhs):
    sweep_apply(cov, lhs, rhs, cov.shape[0] - W)


def row_mean(x):
    return jnp.sum(x, axis=1, keepdims=True) * (1.0 / x.shape[1])


def covariance(anom2, var_ref, cov):
    size, members = anom2[0].shape
    r_ids = lax.broadcasted_iota(jnp.int32, (size, size), 0)
    c_ids = lax.broadcasted_iota(jnp.int32, (size, size), 1)
    full = dot3(anom2, anom2, NT) * (1.0 / (members - 1.0))
    cov[...] = full + jnp.where(r_ids == c_ids, jnp.broadcast_to(var_ref, (size, size)), 0.0)


def column_of(row, eye):
    return jnp.sum(jnp.where(eye, jnp.broadcast_to(row, eye.shape), 0.0), axis=1, keepdims=True)


def eye_of(count):
    return (lax.broadcasted_iota(jnp.int32, (count, count), 0)
            == lax.broadcasted_iota(jnp.int32, (count, count), 1))


def widen(values, count):
    lane = lax.broadcasted_iota(jnp.int32, (1, count), 1)
    wide = count // len(values)
    out = jnp.zeros((1, count), F32)
    for j, value in enumerate(values):
        out = jnp.where((lane >= j * wide) & (lane < (j + 1) * wide), value, out)
    return out


def taper_of(position, where, mask, local_len):
    return mask * jnp.exp(-jnp.abs(position - where) / local_len)


def my_positions(rows, count, ncols):
    first = (lax.axis_index("row") * ncols + lax.axis_index("col")) * rows
    return (first + lax.broadcasted_iota(jnp.int32, (rows, count), 0)).astype(F32)


def gain_of(anom2, obs2, neg_inv2, taper, members):
    cross = dot3(anom2, obs2, NT) * (1.0 / (members - 1.0))
    return split2(dot3(split2(taper * cross), neg_inv2, NN))


def first_batch(nrows, ncols, g_ref, x_ref, rows_ref, owner_ref, mask_ref, val_ref, var_ref,
                inv_ref, x1_ref, anom_hi, anom_lo, push_hi, push_lo, aux_ref, lhs, rhs, beside):
    rows, members = x_ref.shape
    count = rows_ref.shape[1]
    nblk = mask_ref.shape[2]
    local_len = float(rows * nrows * ncols // 4)
    g0 = g_ref[0].reshape(count, members)
    m0 = row_mean(g0)
    a0 = g0 - m0
    anom_hi[...], anom_lo[...] = split2(a0)
    covariance((anom_hi[...], anom_lo[...]), var_ref[0:1, :], inv_ref)
    beside(0)
    lane = lax.broadcasted_iota(jnp.int32, (1, count), 1)
    device = jnp.zeros((1, count), jnp.int32)
    for c in range(1, ncols):
        device = device + jnp.where(lane >= c * (count // ncols), 1, 0)
    for b in range(2):
        aux_ref[b:b + 1, :] = ((owner_ref[b] * ncols + device) * rows + rows_ref[b:b + 1, :]).astype(F32)
        aux_ref[2 + b:3 + b, :] = widen([mask_ref[b, 0, j].astype(F32) for j in range(nblk)], count)
    aux_ref[4:6, :] = val_ref[...]
    aux_ref[6:8, :] = var_ref[...]
    push_hi[...], push_lo[...] = split2(column_of(val_ref[0:1, :], eye_of(count)) - m0 - 0.5 * a0)
    steps = count // W
    cuts = [0, steps // 4, steps // 2, 13 * steps // 16, steps]
    panel = sweep_begin(inv_ref, lhs, rhs)
    for k in range(4):
        panel = sweep_steps(inv_ref, lhs, rhs, panel, cuts[k], cuts[k + 1])
        beside(k + 1)
    sweep_end(inv_ref, lhs, rhs)
    x = x_ref[...]
    taper = taper_of(my_positions(rows, count, ncols), aux_ref[0:1, :], aux_ref[2:3, :], local_len)
    gain = gain_of(split2(x - row_mean(x)), (anom_hi[...], anom_lo[...]), split2(inv_ref[...]), taper, members)
    x1_ref[...] = x - dot3(gain, (push_hi[...], push_lo[...]), NN)
    beside(5)


def solo_kernel(nrows, ncols, *refs):
    first_batch(nrows, ncols, *refs, lambda stage: None)


def flip(index, bits):
    bit = 1
    while bit <= bits:
        if bits & bit:
            index = index + bit - 2 * bit * ((index // bit) % 2)
        bit *= 2
    return index


def share_kernel(nrows, ncols, x_hbm, rows_hbm, owner_hbm, mask_hbm, val_hbm, var_hbm, g_ref, note_ref,
                 inv_ref, x1_ref, anom_hi, anom_lo, push_hi, push_lo, aux_ref,
                 lhs, rhs, x_ref, rows_ref, owner_ref, mask_ref, val_ref, var_ref, load, src, core_slot, part, slots,
                 note_src, note_slots, core_s, core_r, sum_s, sum_r, line_s, line_r, plane_s, plane_r, pair_s, pair_r,
                 nsum_s, nsum_r, nline_s, nline_r):
    loads = [pltpu.make_async_copy(source, target, load.at[k]) for k, (source, target) in enumerate((
        (x_hbm, x_ref), (rows_hbm, rows_ref), (owner_hbm, owner_ref), (mask_hbm, mask_ref),
        (val_hbm, val_ref), (var_hbm, var_ref)))]
    for copy in loads:
        copy.start()
    me = lax.axis_index("row")
    col = lax.axis_index("col")
    nstate, members = x_ref.shape
    count = rows_ref.shape[1]
    per_dev = count // ncols
    q = per_dev // nrows
    half = nrows // 2
    core = me % 2
    chip = me // 2
    sibling = flip(me, 1)
    beside_x = flip(me, 2)
    beside_y = flip(me, 4)
    across = flip(me, 6)
    cut = members // 2

    barrier = pltpu.get_barrier_semaphore()
    for d in range(1, nrows):
        pl.semaphore_signal(barrier, inc=1, device_id=(flip(me, d), col), device_id_type=MESH)
    for d in range(1, ncols):
        pl.semaphore_signal(barrier, inc=1, device_id=(me, flip(col, d)), device_id_type=MESH)

    sent = []

    def put(source, target, send, recv, row, column):
        copy = pltpu.make_async_remote_copy(
            src_ref=source, dst_ref=target, send_sem=send, recv_sem=recv,
            device_id=(row, column), device_id_type=MESH)
        copy.start()
        sent.append(copy)
        return copy

    def same(ref, send, recv, row):
        return put(ref, ref, send, recv, row, col)

    for copy in loads:
        copy.wait()
    x3 = split3(x_ref[...])
    state_ids = lax.broadcasted_iota(jnp.int32, (nstate, per_dev), 0)

    def select(b):
        ids = jnp.broadcast_to(rows_ref[b:b + 1, :], (8, count))
        ids = pltpu.roll(ids, (count - col * per_dev) % count, 1)[0:1, :per_dev]
        here = jnp.full((1, per_dev), owner_ref[b], jnp.int32) == me
        ids = jnp.where(here, ids, -1)
        pick = jnp.where(ids == state_ids, 1.0, 0.0).astype(BF16)
        rows = (mm(pick, x3[0], TN) + mm(pick, x3[1], TN)) + mm(pick, x3[2], TN)
        src[b] = rows.reshape(half, 2, q, members)

    def to_core(b):
        return put(src.at[b, :, 1 - core], core_slot.at[b], core_s.at[b], core_r.at[b], sibling, col)

    def to_chips(b, copy):
        copy.wait_recv()
        part[b] = src[b, :, core] + core_slot[b]
        return [put(part.at[b, flip(chip, d)], slots.at[b, d - 1], sum_s.at[b, d - 1], sum_r.at[b, d - 1],
                    flip(me, 2 * d), col) for d in range(1, half)]

    def along_line(b, copies):
        for copy in copies:
            copy.wait_recv()
        total = part[b, chip]
        for d in range(1, half):
            total = total + slots[b, d - 1]
        g_ref[b, col, me] = total
        mine = g_ref.at[b, col, me]
        return [put(mine, mine, line_s.at[b, d - 1], line_r.at[b, d - 1], me, flip(col, d))
                for d in range(1, ncols)]

    def spread(b, d):
        slab = g_ref.at[b, flip(col, d), me]
        x_copy = same(slab, plane_s.at[b, d, 0], plane_r.at[b, d, 0], beside_x)
        y_copy = same(slab, plane_s.at[b, d, 1], plane_r.at[b, d, 1], beside_y)
        return [x_copy, y_copy], [same(slab, pair_s.at[b, d, 0], pair_r.at[b, d, 0], sibling)]

    def spread_lines(b, lines, first):
        planes, pairs = [first[0]], list(first[1])
        for d in range(1, ncols):
            lines[d - 1].wait_recv()
            more = spread(b, d)
            planes.append(more[0])
            pairs.extend(more[1])
        return planes, pairs

    def relay(b, d, planes, pairs):
        planes[d][0].wait_recv()
        slab = g_ref.at[b, flip(col, d), beside_x]
        planes[d].append(same(slab.at[:, :cut], plane_s.at[b, d, 2], plane_r.at[b, d, 2], beside_y))
        pairs.append(same(slab, pair_s.at[b, d, 1], pair_r.at[b, d, 1], sibling))
        planes[d][1].wait_recv()
        slab = g_ref.at[b, flip(col, d), beside_y]
        planes[d].append(same(slab.at[:, cut:], plane_s.at[b, d, 3], plane_r.at[b, d, 3], beside_x))
        pairs.append(same(slab, pair_s.at[b, d, 2], pair_r.at[b, d, 2], sibling))

    def relay_all(b, planes, pairs):
        for d in range(ncols):
            relay(b, d, planes, pairs)

    def finish(b, planes, pairs):
        for d in range(ncols):
            planes[d][2].wait_recv()
            planes[d][3].wait_recv()
            pairs.append(same(g_ref.at[b, flip(col, d), across], pair_s.at[b, d, 3], pair_r.at[b, d, 3], sibling))

    lane = lax.broadcasted_iota(jnp.int32, (8, 128), 1)
    note = jnp.zeros((8, 128), F32)
    for j in range(mask_ref.shape[2]):
        note = jnp.where(lane == j, mask_ref[0, 0, j].astype(F32), note)
    here = jnp.full((8, 128), owner_ref[1], jnp.int32) == me
    note_src[...] = jnp.where(here, note, 0.0)
    select(0)
    pl.semaphore_wait(barrier, nrows + ncols - 2)
    core0 = to_core(0)
    select(1)
    core1 = to_core(1)
    sums0 = to_chips(0, core0)
    lines0 = along_line(0, sums0)
    first0 = spread(0, 0)
    sums1 = to_chips(1, core1)
    notes = [put(note_src, note_slots.at[d - 1], nsum_s.at[d - 1], nsum_r.at[d - 1], flip(me, d), col)
             for d in range(1, nrows)]
    planes0, pairs0 = spread_lines(0, lines0, first0)
    lines1 = along_line(1, sums1)
    later = [lines1, spread(1, 0)]
    relay_all(0, planes0, pairs0)
    finish(0, planes0, pairs0)
    total = note_src[...]
    for d in range(1, nrows):
        notes[d - 1].wait_recv()
        total = total + note_slots[d - 1]
    note_ref[col] = total
    note_lines = [put(note_ref.at[col], note_ref.at[col], nline_s.at[d - 1], nline_r.at[d - 1], me, flip(col, d))
                  for d in range(1, ncols)]
    for copy in pairs0:
        copy.wait_recv()

    def beside(stage):
        if stage == 0:
            later[:] = spread_lines(1, *later)
        elif stage == 1:
            relay_all(1, *later)
        elif stage == 2:
            finish(1, *later)
        elif stage == 5:
            for copy in later[1] + note_lines:
                copy.wait_recv()

    first_batch(nrows, ncols, g_ref, x_ref, rows_ref, owner_ref, mask_ref, val_ref, var_ref,
                inv_ref, x1_ref, anom_hi, anom_lo, push_hi, push_lo, aux_ref, lhs, rhs, beside)
    for copy in sent:
        copy.wait_send()


def second_kernel(nrows, ncols, nblk, g_ref, note_ref, inv_ref, x1_ref, anom_hi, anom_lo, push_hi, push_lo, aux_ref,
                  out_ref, g1, cov, lhs, rhs):
    rows, members = x1_ref.shape
    count = inv_ref.shape[0]
    local_len = float(rows * nrows * ncols // 4)
    eye = eye_of(count)
    mask_g = jnp.concatenate(
        [jnp.broadcast_to(widen([note_ref[c, 0:1, j:j + 1] for j in range(nblk)], count), (count // ncols, count))
         for c in range(ncols)], axis=0)
    taper = taper_of(column_of(aux_ref[1:2, :], eye), aux_ref[0:1, :], mask_g, local_len)
    g = g_ref[1].reshape(count, members)
    gain = gain_of(split2(g - row_mean(g)), (anom_hi[...], anom_lo[...]), split2(inv_ref[...]), taper, members)
    g1[...] = g - dot3(gain, (push_hi[...], push_lo[...]), NN)
    g = g1[...]
    m1 = row_mean(g)
    a1 = g - m1
    a12 = split2(a1)
    covariance(a12, aux_ref[7:8, :], cov)
    panel = sweep_begin(cov, lhs, rhs)
    sweep_steps(cov, lhs, rhs, panel, 0, count // W)
    sweep_end(cov, lhs, rhs)
    push = split2(column_of(aux_ref[5:6, :], eye) - m1 - 0.5 * a1)
    x = x1_ref[...]
    taper = taper_of(my_positions(rows, count, ncols), aux_ref[1:2, :], aux_ref[3:4, :], local_len)
    gain = gain_of(split2(x - row_mean(x)), a12, split2(cov[...]), taper, members)
    out_ref[...] = x - dot3(gain, push, NN)


def shared_by_collectives(ensemble, obs_rows, owner, taper_mask, ncols):
    rows, members = ensemble.shape
    batches, count = obs_rows.shape
    per_dev = count // ncols
    nblk = taper_mask.shape[2]
    my_row = lax.axis_index("row")
    mine = lax.dynamic_slice_in_dim(obs_rows, lax.axis_index("col") * per_dev, per_dev, axis=1)
    row_ids = jnp.arange(rows, dtype=jnp.int32)
    shared = []
    for batch in range(batches):
        here = owner[batch] == my_row
        picker = ((mine[batch][:, None] == row_ids[None, :]) & here).astype(F32)
        part = jnp.dot(picker, ensemble, precision=lax.Precision.HIGHEST)
        shared.append(lax.all_gather(lax.psum(part, "row"), "col", axis=0).reshape(count, members))
    note = jnp.where(owner[1] == my_row, taper_mask[0, 0].astype(F32), 0.0)
    note = jnp.pad(jnp.broadcast_to(note[None, :], (8, nblk)), ((0, 0), (0, 128 - nblk)))
    note = lax.all_gather(lax.psum(note, "row"), "col", axis=0)
    return jnp.stack(shared), note


def on_device(nrows, ncols, ensemble, obs_rows, owner, obs_value, obs_var, taper_mask):
    rows, members = ensemble.shape
    batches, count = obs_rows.shape
    per_dev = count // ncols
    half_shape = jax.ShapeDtypeStruct((count, members), BF16)
    kept = (
        jax.ShapeDtypeStruct((count, count), F32),
        jax.ShapeDtypeStruct((rows, members), F32),
        half_shape, half_shape, half_shape, half_shape,
        jax.ShapeDtypeStruct((8, count), F32),
    )
    limit = 40 * 2**20
    terms = [pltpu.VMEM((6 * W, count), BF16)] * 2
    if nrows == 8 and ncols & (ncols - 1) == 0 and per_dev % (8 * nrows) == 0:
        q = per_dev // nrows
        half = nrows // 2
        dma = pltpu.SemaphoreType.DMA
        shared, note, *held = pl.pallas_call(
            functools.partial(share_kernel, nrows, ncols),
            out_shape=(
                jax.ShapeDtypeStruct((batches, ncols, nrows, q, members), F32),
                jax.ShapeDtypeStruct((ncols, 8, 128), F32),
            ) + kept,
            in_specs=[HBM] * 6,
            out_specs=(VMEM,) * 9,
            scratch_shapes=terms + [
                pltpu.VMEM(ensemble.shape, F32),
                pltpu.VMEM(obs_rows.shape, jnp.int32),
                pltpu.SMEM(owner.shape, jnp.int32),
                pltpu.SMEM(taper_mask.shape, jnp.int32),
                pltpu.VMEM(obs_value.shape, F32),
                pltpu.VMEM(obs_var.shape, F32),
                dma((6,)),
                pltpu.VMEM((batches, half, 2, q, members), F32),
                pltpu.VMEM((batches, half, q, members), F32),
                pltpu.VMEM((batches, half, q, members), F32),
                pltpu.VMEM((batches, half - 1, q, members), F32),
                pltpu.VMEM((8, 128), F32),
                pltpu.VMEM((nrows - 1, 8, 128), F32),
            ] + [dma((batches,))] * 2 + [dma((batches, half - 1))] * 2 + [dma((batches, ncols - 1))] * 2
            + [dma((batches, ncols, 4))] * 4 + [dma((nrows - 1,))] * 2 + [dma((ncols - 1,))] * 2,
            compiler_params=pltpu.CompilerParams(
                vmem_limit_bytes=limit, collective_id=0, has_side_effects=True),
        )(*[pltpu.with_memory_space_constraint(arg, pltpu.HBM)
            for arg in (ensemble, obs_rows, owner, taper_mask, obs_value, obs_var)])
    else:
        shared, note = shared_by_collectives(ensemble, obs_rows, owner, taper_mask, ncols)
        held = pl.pallas_call(
            functools.partial(solo_kernel, nrows, ncols),
            out_shape=kept,
            in_specs=[VMEM] * 3 + [SMEM] * 2 + [VMEM] * 2,
            out_specs=(VMEM,) * 7,
            scratch_shapes=terms,
            compiler_params=pltpu.CompilerParams(vmem_limit_bytes=limit),
        )(shared, ensemble, obs_rows, owner, taper_mask, obs_value, obs_var)
    return pl.pallas_call(
        functools.partial(second_kernel, nrows, ncols, taper_mask.shape[2]),
        out_shape=jax.ShapeDtypeStruct((rows, members), F32),
        in_specs=[VMEM] * 9,
        out_specs=VMEM,
        scratch_shapes=[pltpu.VMEM((count, members), F32), pltpu.VMEM((count, count), F32)] + terms,
        compiler_params=pltpu.CompilerParams(vmem_limit_bytes=limit),
    )(shared, note, *held)


def solution(mesh):
    in_specs = (P(("row", "col"), None), P(), P(), P(), P(), P(None, ("row", "col"), None))
    out_specs = P(("row", "col"), None)
    return jax.shard_map(
        functools.partial(on_device, mesh.shape["row"], mesh.shape["col"]),
        mesh=mesh, in_specs=in_specs, out_specs=out_specs, check_vma=False
    )
```

```python
import functools

import jax
import jax.numpy as jnp
from jax import lax
from jax.experimental import pallas as pl
from jax.experimental.pallas import tpu as pltpu
from jax.sharding import PartitionSpec as P

W = 16
F32 = jnp.float32
BF16 = jnp.bfloat16
NN = (((1,), (0,)), ((), ()))
NT = (((1,), (1,)), ((), ()))
TN = (((0,), (0,)), ((), ()))
MESH = pl.DeviceIdType.MESH
VMEM = pl.BlockSpec(memory_space=pltpu.VMEM)
SMEM = pl.BlockSpec(memory_space=pltpu.SMEM)
HBM = pl.BlockSpec(memory_space=pltpu.HBM)


def split2(x):
    hi = x.astype(BF16)
    return hi, (x - hi.astype(F32)).astype(BF16)


def split3(x):
    hi = x.astype(BF16)
    rest = x - hi.astype(F32)
    mid = rest.astype(BF16)
    return hi, mid, (rest - mid.astype(F32)).astype(BF16)


def mm(a, b, dims):
    return lax.dot_general(a, b, dims, preferred_element_type=F32)


def dot3(a, b, dims):
    return mm(a[0], b[0], dims) + (mm(a[0], b[1], dims) + mm(a[1], b[0], dims))


def sweep_inverse(cov, begin=0, end=None):
    size = cov.shape[0]
    lane = lax.broadcasted_iota(jnp.int32, (W, size), 1)
    row = lax.broadcasted_iota(jnp.int32, (W, size), 0)
    row_small = lax.broadcasted_iota(jnp.int32, (W, 128), 0)

    def body(k, carry):
        start = pl.multiple_of(k * W, W)
        panel = cov[pl.ds(start, W), :]
        rolled = pltpu.roll(panel, size - start, 1)
        cols = [jnp.broadcast_to(rolled[:, i:i + 1], (W, 128)) for i in range(W)]
        inside = (lane >= start) & (lane < start + W)
        left = jnp.where(inside, jnp.where(lane - start == row, -1.0, 0.0), panel)
        right = left
        scale = jnp.zeros((W, 128), F32)
        for j in range(W):
            inv = 1.0 / cols[j][j:j + 1, :]
            here = row_small == j
            mult = jnp.where(here, 0.0, cols[j])
            scale = jnp.where(here, inv, scale)
            for i in range(j + 1, W):
                cols[i] = cols[i] - mult * (cols[i][j:j + 1, :] * inv)
            wide = jnp.concatenate([mult] * (size // 128), axis=1)
            wide_inv = jnp.concatenate([inv] * (size // 128), axis=1)
            right = right - wide * (right[j:j + 1, :] * wide_inv)
        right = right * jnp.concatenate([scale] * (size // 128), axis=1)
        a1, a2, a3 = split3(left)
        b1, b2, b3 = split3(right)
        lhs = jnp.concatenate([a1, a1, a2, a1, a2, a3], axis=0)
        rhs = jnp.concatenate([b1, b2, b1, b3, b2, b1], axis=0)
        change = mm(lhs, rhs, TN)
        r_ids = lax.broadcasted_iota(jnp.int32, (size, size), 0)
        c_ids = lax.broadcasted_iota(jnp.int32, (size, size), 1)
        hit = ((r_ids >= start) & (r_ids < start + W)) | ((c_ids >= start) & (c_ids < start + W))
        cov[...] = jnp.where(hit, 0.0, cov[...]) - change
        return carry

    lax.fori_loop(begin, size // W if end is None else end, body, 0)


def row_mean(x):
    return jnp.sum(x, axis=1, keepdims=True) * (1.0 / x.shape[1])


def covariance(anom2, var_ref, cov):
    size, members = anom2[0].shape
    r_ids = lax.broadcasted_iota(jnp.int32, (size, size), 0)
    c_ids = lax.broadcasted_iota(jnp.int32, (size, size), 1)
    full = dot3(anom2, anom2, NT) * (1.0 / (members - 1.0))
    cov[...] = full + jnp.where(r_ids == c_ids, jnp.broadcast_to(var_ref, (size, size)), 0.0)


def column_of(row, eye):
    return jnp.sum(jnp.where(eye, jnp.broadcast_to(row, eye.shape), 0.0), axis=1, keepdims=True)


def eye_of(count):
    return (lax.broadcasted_iota(jnp.int32, (count, count), 0)
            == lax.broadcasted_iota(jnp.int32, (count, count), 1))


def widen(values, count):
    lane = lax.broadcasted_iota(jnp.int32, (1, count), 1)
    wide = count // len(values)
    out = jnp.zeros((1, count), F32)
    for j, value in enumerate(values):
        out = jnp.where((lane >= j * wide) & (lane < (j + 1) * wide), value, out)
    return out


def taper_of(position, where, mask, local_len):
    return mask * jnp.exp(-jnp.abs(position - where) / local_len)


def my_positions(rows, count, ncols):
    first = (lax.axis_index("row") * ncols + lax.axis_index("col")) * rows
    return (first + lax.broadcasted_iota(jnp.int32, (rows, count), 0)).astype(F32)


def gain_of(anom2, obs2, neg_inv2, taper, members):
    cross = dot3(anom2, obs2, NT) * (1.0 / (members - 1.0))
    return split2(dot3(split2(taper * cross), neg_inv2, NN))


def first_batch(nrows, ncols, g_ref, x_ref, rows_ref, owner_ref, mask_ref, val_ref, var_ref,
                inv_ref, x1_ref, anom_hi, anom_lo, push_hi, push_lo, aux_ref, beside):
    rows, members = x_ref.shape
    count = rows_ref.shape[1]
    nblk = mask_ref.shape[2]
    local_len = float(rows * nrows * ncols // 4)
    g0 = g_ref[0].reshape(count, members)
    m0 = row_mean(g0)
    a0 = g0 - m0
    anom_hi[...], anom_lo[...] = split2(a0)
    covariance((anom_hi[...], anom_lo[...]), var_ref[0:1, :], inv_ref)
    beside(0)
    lane = lax.broadcasted_iota(jnp.int32, (1, count), 1)
    device = jnp.zeros((1, count), jnp.int32)
    for c in range(1, ncols):
        device = device + jnp.where(lane >= c * (count // ncols), 1, 0)
    for b in range(2):
        aux_ref[b:b + 1, :] = ((owner_ref[b] * ncols + device) * rows + rows_ref[b:b + 1, :]).astype(F32)
        aux_ref[2 + b:3 + b, :] = widen([mask_ref[b, 0, j].astype(F32) for j in range(nblk)], count)
    aux_ref[4:6, :] = val_ref[...]
    aux_ref[6:8, :] = var_ref[...]
    push_hi[...], push_lo[...] = split2(column_of(val_ref[0:1, :], eye_of(count)) - m0 - 0.5 * a0)
    steps = count // W
    cuts = [0, steps // 4, 5 * steps // 8, steps]
    for k in range(3):
        sweep_inverse(inv_ref, cuts[k], cuts[k + 1])
        beside(k + 1)
    x = x_ref[...]
    taper = taper_of(my_positions(rows, count, ncols), aux_ref[0:1, :], aux_ref[2:3, :], local_len)
    gain = gain_of(split2(x - row_mean(x)), (anom_hi[...], anom_lo[...]), split2(inv_ref[...]), taper, members)
    x1_ref[...] = x - dot3(gain, (push_hi[...], push_lo[...]), NN)
    beside(5)


def solo_kernel(nrows, ncols, *refs):
    first_batch(nrows, ncols, *refs, lambda stage: None)


def flip(index, bits):
    bit = 1
    while bit <= bits:
        if bits & bit:
            index = index + bit - 2 * bit * ((index // bit) % 2)
        bit *= 2
    return index


def share_kernel(nrows, ncols, x_hbm, rows_hbm, owner_hbm, mask_hbm, val_hbm, var_hbm, g_ref, note_ref,
                 inv_ref, x1_ref, anom_hi, anom_lo, push_hi, push_lo, aux_ref,
                 x_ref, rows_ref, owner_ref, mask_ref, val_ref, var_ref, load, src, core_slot, part, slots,
                 note_src, note_slots, core_s, core_r, sum_s, sum_r, line_s, line_r, plane_s, plane_r, pair_s, pair_r,
                 nsum_s, nsum_r, nline_s, nline_r):
    loads = [pltpu.make_async_copy(source, target, load.at[k]) for k, (source, target) in enumerate((
        (x_hbm, x_ref), (rows_hbm, rows_ref), (owner_hbm, owner_ref), (mask_hbm, mask_ref),
        (val_hbm, val_ref), (var_hbm, var_ref)))]
    for copy in loads:
        copy.start()
    me = lax.axis_index("row")
    col = lax.axis_index("col")
    nstate, members = x_ref.shape
    count = rows_ref.shape[1]
    per_dev = count // ncols
    q = per_dev // nrows
    half = nrows // 2
    core = me % 2
    chip = me // 2
    sibling = flip(me, 1)
    beside_x = flip(me, 2)
    beside_y = flip(me, 4)
    across = flip(me, 6)
    cut = members // 2

    barrier = pltpu.get_barrier_semaphore()
    for d in range(1, nrows):
        pl.semaphore_signal(barrier, inc=1, device_id=(flip(me, d), col), device_id_type=MESH)
    for d in range(1, ncols):
        pl.semaphore_signal(barrier, inc=1, device_id=(me, flip(col, d)), device_id_type=MESH)

    sent = []

    def put(source, target, send, recv, row, column):
        copy = pltpu.make_async_remote_copy(
            src_ref=source, dst_ref=target, send_sem=send, recv_sem=recv,
            device_id=(row, column), device_id_type=MESH)
        copy.start()
        sent.append(copy)
        return copy

    def same(ref, send, recv, row):
        return put(ref, ref, send, recv, row, col)

    for copy in loads:
        copy.wait()
    x3 = split3(x_ref[...])
    state_ids = lax.broadcasted_iota(jnp.int32, (nstate, per_dev), 0)

    def select(b):
        ids = jnp.broadcast_to(rows_ref[b:b + 1, :], (8, count))
        ids = pltpu.roll(ids, (count - col * per_dev) % count, 1)[0:1, :per_dev]
        here = jnp.full((1, per_dev), owner_ref[b], jnp.int32) == me
        ids = jnp.where(here, ids, -1)
        pick = jnp.where(ids == state_ids, 1.0, 0.0).astype(BF16)
        rows = (mm(pick, x3[0], TN) + mm(pick, x3[1], TN)) + mm(pick, x3[2], TN)
        src[b] = rows.reshape(half, 2, q, members)

    def to_core(b):
        return put(src.at[b, :, 1 - core], core_slot.at[b], core_s.at[b], core_r.at[b], sibling, col)

    def to_chips(b, copy):
        copy.wait_recv()
        part[b] = src[b, :, core] + core_slot[b]
        return [put(part.at[b, flip(chip, d)], slots.at[b, d - 1], sum_s.at[b, d - 1], sum_r.at[b, d - 1],
                    flip(me, 2 * d), col) for d in range(1, half)]

    def along_line(b, copies):
        for copy in copies:
            copy.wait_recv()
        total = part[b, chip]
        for d in range(1, half):
            total = total + slots[b, d - 1]
        g_ref[b, col, me] = total
        mine = g_ref.at[b, col, me]
        return [put(mine, mine, line_s.at[b, d - 1], line_r.at[b, d - 1], me, flip(col, d))
                for d in range(1, ncols)]

    def spread(b, d):
        slab = g_ref.at[b, flip(col, d), me]
        x_copy = same(slab, plane_s.at[b, d, 0], plane_r.at[b, d, 0], beside_x)
        y_copy = same(slab, plane_s.at[b, d, 1], plane_r.at[b, d, 1], beside_y)
        return [x_copy, y_copy], [same(slab, pair_s.at[b, d, 0], pair_r.at[b, d, 0], sibling)]

    def spread_lines(b, lines, first):
        planes, pairs = [first[0]], list(first[1])
        for d in range(1, ncols):
            lines[d - 1].wait_recv()
            more = spread(b, d)
            planes.append(more[0])
            pairs.extend(more[1])
        return planes, pairs

    def relay(b, d, planes, pairs):
        planes[d][0].wait_recv()
        slab = g_ref.at[b, flip(col, d), beside_x]
        planes[d].append(same(slab.at[:, :cut], plane_s.at[b, d, 2], plane_r.at[b, d, 2], beside_y))
        pairs.append(same(slab, pair_s.at[b, d, 1], pair_r.at[b, d, 1], sibling))
        planes[d][1].wait_recv()
        slab = g_ref.at[b, flip(col, d), beside_y]
        planes[d].append(same(slab.at[:, cut:], plane_s.at[b, d, 3], plane_r.at[b, d, 3], beside_x))
        pairs.append(same(slab, pair_s.at[b, d, 2], pair_r.at[b, d, 2], sibling))

    def relay_all(b, planes, pairs):
        for d in range(ncols):
            relay(b, d, planes, pairs)

    def finish(b, planes, pairs):
        for d in range(ncols):
            planes[d][2].wait_recv()
            planes[d][3].wait_recv()
            pairs.append(same(g_ref.at[b, flip(col, d), across], pair_s.at[b, d, 3], pair_r.at[b, d, 3], sibling))

    lane = lax.broadcasted_iota(jnp.int32, (8, 128), 1)
    note = jnp.zeros((8, 128), F32)
    for j in range(mask_ref.shape[2]):
        note = jnp.where(lane == j, mask_ref[0, 0, j].astype(F32), note)
    here = jnp.full((8, 128), owner_ref[1], jnp.int32) == me
    note_src[...] = jnp.where(here, note, 0.0)
    select(0)
    pl.semaphore_wait(barrier, nrows + ncols - 2)
    core0 = to_core(0)
    select(1)
    core1 = to_core(1)
    sums0 = to_chips(0, core0)
    lines0 = along_line(0, sums0)
    first0 = spread(0, 0)
    sums1 = to_chips(1, core1)
    notes = [put(note_src, note_slots.at[d - 1], nsum_s.at[d - 1], nsum_r.at[d - 1], flip(me, d), col)
             for d in range(1, nrows)]
    planes0, pairs0 = spread_lines(0, lines0, first0)
    lines1 = along_line(1, sums1)
    later = [lines1, spread(1, 0)]
    relay_all(0, planes0, pairs0)
    finish(0, planes0, pairs0)
    total = note_src[...]
    for d in range(1, nrows):
        notes[d - 1].wait_recv()
        total = total + note_slots[d - 1]
    note_ref[col] = total
    note_lines = [put(note_ref.at[col], note_ref.at[col], nline_s.at[d - 1], nline_r.at[d - 1], me, flip(col, d))
                  for d in range(1, ncols)]
    for copy in pairs0:
        copy.wait_recv()

    def beside(stage):
        if stage == 0:
            later[:] = spread_lines(1, *later)
        elif stage == 1:
            relay_all(1, *later)
        elif stage == 2:
            finish(1, *later)
        elif stage == 5:
            for copy in later[1] + note_lines:
                copy.wait_recv()

    first_batch(nrows, ncols, g_ref, x_ref, rows_ref, owner_ref, mask_ref, val_ref, var_ref,
                inv_ref, x1_ref, anom_hi, anom_lo, push_hi, push_lo, aux_ref, beside)
    for copy in sent:
        copy.wait_send()


def second_kernel(nrows, ncols, nblk, g_ref, note_ref, inv_ref, x1_ref, anom_hi, anom_lo, push_hi, push_lo, aux_ref,
                  out_ref, g1, cov):
    rows, members = x1_ref.shape
    count = inv_ref.shape[0]
    local_len = float(rows * nrows * ncols // 4)
    eye = eye_of(count)
    mask_g = jnp.concatenate(
        [jnp.broadcast_to(widen([note_ref[c, 0:1, j:j + 1] for j in range(nblk)], count), (count // ncols, count))
         for c in range(ncols)], axis=0)
    taper = taper_of(column_of(aux_ref[1:2, :], eye), aux_ref[0:1, :], mask_g, local_len)
    g = g_ref[1].reshape(count, members)
    gain = gain_of(split2(g - row_mean(g)), (anom_hi[...], anom_lo[...]), split2(inv_ref[...]), taper, members)
    g1[...] = g - dot3(gain, (push_hi[...], push_lo[...]), NN)
    g = g1[...]
    m1 = row_mean(g)
    a1 = g - m1
    a12 = split2(a1)
    covariance(a12, aux_ref[7:8, :], cov)
    sweep_inverse(cov)
    push = split2(column_of(aux_ref[5:6, :], eye) - m1 - 0.5 * a1)
    x = x1_ref[...]
    taper = taper_of(my_positions(rows, count, ncols), aux_ref[1:2, :], aux_ref[3:4, :], local_len)
    gain = gain_of(split2(x - row_mean(x)), a12, split2(cov[...]), taper, members)
    out_ref[...] = x - dot3(gain, push, NN)


def shared_by_collectives(ensemble, obs_rows, owner, taper_mask, ncols):
    rows, members = ensemble.shape
    batches, count = obs_rows.shape
    per_dev = count // ncols
    nblk = taper_mask.shape[2]
    my_row = lax.axis_index("row")
    mine = lax.dynamic_slice_in_dim(obs_rows, lax.axis_index("col") * per_dev, per_dev, axis=1)
    row_ids = jnp.arange(rows, dtype=jnp.int32)
    shared = []
    for batch in range(batches):
        here = owner[batch] == my_row
        picker = ((mine[batch][:, None] == row_ids[None, :]) & here).astype(F32)
        part = jnp.dot(picker, ensemble, precision=lax.Precision.HIGHEST)
        shared.append(lax.all_gather(lax.psum(part, "row"), "col", axis=0).reshape(count, members))
    note = jnp.where(owner[1] == my_row, taper_mask[0, 0].astype(F32), 0.0)
    note = jnp.pad(jnp.broadcast_to(note[None, :], (8, nblk)), ((0, 0), (0, 128 - nblk)))
    note = lax.all_gather(lax.psum(note, "row"), "col", axis=0)
    return jnp.stack(shared), note


def on_device(nrows, ncols, ensemble, obs_rows, owner, obs_value, obs_var, taper_mask):
    rows, members = ensemble.shape
    batches, count = obs_rows.shape
    per_dev = count // ncols
    half_shape = jax.ShapeDtypeStruct((count, members), BF16)
    kept = (
        jax.ShapeDtypeStruct((count, count), F32),
        jax.ShapeDtypeStruct((rows, members), F32),
        half_shape, half_shape, half_shape, half_shape,
        jax.ShapeDtypeStruct((8, count), F32),
    )
    limit = 40 * 2**20
    if nrows == 8 and ncols & (ncols - 1) == 0 and per_dev % (8 * nrows) == 0:
        q = per_dev // nrows
        half = nrows // 2
        dma = pltpu.SemaphoreType.DMA
        shared, note, *held = pl.pallas_call(
            functools.partial(share_kernel, nrows, ncols),
            out_shape=(
                jax.ShapeDtypeStruct((batches, ncols, nrows, q, members), F32),
                jax.ShapeDtypeStruct((ncols, 8, 128), F32),
            ) + kept,
            in_specs=[HBM] * 6,
            out_specs=(VMEM,) * 9,
            scratch_shapes=[
                pltpu.VMEM(ensemble.shape, F32),
                pltpu.VMEM(obs_rows.shape, jnp.int32),
                pltpu.SMEM(owner.shape, jnp.int32),
                pltpu.SMEM(taper_mask.shape, jnp.int32),
                pltpu.VMEM(obs_value.shape, F32),
                pltpu.VMEM(obs_var.shape, F32),
                dma((6,)),
                pltpu.VMEM((batches, half, 2, q, members), F32),
                pltpu.VMEM((batches, half, q, members), F32),
                pltpu.VMEM((batches, half, q, members), F32),
                pltpu.VMEM((batches, half - 1, q, members), F32),
                pltpu.VMEM((8, 128), F32),
                pltpu.VMEM((nrows - 1, 8, 128), F32),
            ] + [dma((batches,))] * 2 + [dma((batches, half - 1))] * 2 + [dma((batches, ncols - 1))] * 2
            + [dma((batches, ncols, 4))] * 4 + [dma((nrows - 1,))] * 2 + [dma((ncols - 1,))] * 2,
            compiler_params=pltpu.CompilerParams(
                vmem_limit_bytes=limit, collective_id=0, has_side_effects=True),
        )(*[pltpu.with_memory_space_constraint(arg, pltpu.HBM)
            for arg in (ensemble, obs_rows, owner, taper_mask, obs_value, obs_var)])
    else:
        shared, note = shared_by_collectives(ensemble, obs_rows, owner, taper_mask, ncols)
        held = pl.pallas_call(
            functools.partial(solo_kernel, nrows, ncols),
            out_shape=kept,
            in_specs=[VMEM] * 3 + [SMEM] * 2 + [VMEM] * 2,
            out_specs=(VMEM,) * 7,
            compiler_params=pltpu.CompilerParams(vmem_limit_bytes=limit),
        )(shared, ensemble, obs_rows, owner, taper_mask, obs_value, obs_var)
    return pl.pallas_call(
        functools.partial(second_kernel, nrows, ncols, taper_mask.shape[2]),
        out_shape=jax.ShapeDtypeStruct((rows, members), F32),
        in_specs=[VMEM] * 9,
        out_specs=VMEM,
        scratch_shapes=[pltpu.VMEM((count, members), F32), pltpu.VMEM((count, count), F32)],
        compiler_params=pltpu.CompilerParams(vmem_limit_bytes=limit),
    )(shared, note, *held)


def solution(mesh):
    in_specs = (P(("row", "col"), None), P(), P(), P(), P(), P(None, ("row", "col"), None))
    out_specs = P(("row", "col"), None)
    return jax.shard_map(
        functools.partial(on_device, mesh.shape["row"], mesh.shape["col"]),
        mesh=mesh, in_specs=in_specs, out_specs=out_specs, check_vma=False
    )
```

```python
import functools

import jax
import jax.numpy as jnp
from jax import lax
from jax.experimental import pallas as pl
from jax.experimental.pallas import tpu as pltpu
from jax.sharding import PartitionSpec as P

W = 16
F32 = jnp.float32
BF16 = jnp.bfloat16
NN = (((1,), (0,)), ((), ()))
NT = (((1,), (1,)), ((), ()))
TN = (((0,), (0,)), ((), ()))
MESH = pl.DeviceIdType.MESH
VMEM = pl.BlockSpec(memory_space=pltpu.VMEM)
SMEM = pl.BlockSpec(memory_space=pltpu.SMEM)
HBM = pl.BlockSpec(memory_space=pltpu.HBM)


def split2(x):
    hi = x.astype(BF16)
    return hi, (x - hi.astype(F32)).astype(BF16)


def split3(x):
    hi = x.astype(BF16)
    rest = x - hi.astype(F32)
    mid = rest.astype(BF16)
    return hi, mid, (rest - mid.astype(F32)).astype(BF16)


def mm(a, b, dims):
    return lax.dot_general(a, b, dims, preferred_element_type=F32)


def dot3(a, b, dims):
    return mm(a[0], b[0], dims) + (mm(a[0], b[1], dims) + mm(a[1], b[0], dims))


def sweep_inverse(cov, rhs, begin=0, end=None):
    size = cov.shape[0]
    lane = lax.broadcasted_iota(jnp.int32, (W, size), 1)
    row = lax.broadcasted_iota(jnp.int32, (W, size), 0)
    line = lax.broadcasted_iota(jnp.int32, (1, size), 1)
    if begin == 0:
        rhs[...] = jnp.zeros(rhs.shape, BF16)
    row_small = lax.broadcasted_iota(jnp.int32, (W, 128), 0)

    def body(k, carry):
        start = pl.multiple_of(k * W, W)
        panel = cov[pl.ds(start, W), :]
        rolled = pltpu.roll(panel, size - start, 1)
        cols = [jnp.broadcast_to(rolled[:, i:i + 1], (W, 128)) for i in range(W)]
        inside = (lane >= start) & (lane < start + W)
        left = jnp.where(inside, jnp.where(lane - start == row, -1.0, 0.0), panel)
        group = pl.multiple_of((start // 128) * 128, 128)
        cov[pl.ds(start, W), :] = jnp.where(inside, left, 0.0)
        own = line[:, :128] + group
        a1, a2, a3 = split3(jnp.where((own >= start) & (own < start + W), cov[:, pl.ds(group, 128)], 0.0))
        lhs = [jnp.concatenate(two, axis=1) for two in ((a1, a1), (a2, a1), (a2, a3))]
        right = left
        scale = jnp.zeros((W, 128), F32)
        for j in range(W):
            inv = 1.0 / cols[j][j:j + 1, :]
            here = row_small == j
            mult = jnp.where(here, 0.0, cols[j])
            scale = jnp.where(here, inv, scale)
            for i in range(j + 1, W):
                cols[i] = cols[i] - mult * (cols[i][j:j + 1, :] * inv)
            wide = jnp.concatenate([mult] * (size // 128), axis=1)
            wide_inv = jnp.concatenate([inv] * (size // 128), axis=1)
            right = right - wide * (right[j:j + 1, :] * wide_inv)
        right = right * jnp.concatenate([scale] * (size // 128), axis=1)
        for t, term in enumerate(split3(right)):
            rhs[t, pl.ds(pl.multiple_of(start - group, W), W), :] = term
        b1, b2, b3 = rhs[0], rhs[1], rhs[2]
        change = (mm(lhs[0], jnp.concatenate([b1, b2], axis=0), NN)
                  + (mm(lhs[1], jnp.concatenate([b1, b3], axis=0), NN)
                     + mm(lhs[2], jnp.concatenate([b2, b1], axis=0), NN)))
        cov[...] = jnp.where((line >= start) & (line < start + W), 0.0, cov[...]) - change
        return carry

    lax.fori_loop(begin, size // W if end is None else end, body, 0)


def row_mean(x):
    return jnp.sum(x, axis=1, keepdims=True) * (1.0 / x.shape[1])


def covariance(anom2, var_ref, cov):
    size, members = anom2[0].shape
    r_ids = lax.broadcasted_iota(jnp.int32, (size, size), 0)
    c_ids = lax.broadcasted_iota(jnp.int32, (size, size), 1)
    full = dot3(anom2, anom2, NT) * (1.0 / (members - 1.0))
    cov[...] = full + jnp.where(r_ids == c_ids, jnp.broadcast_to(var_ref, (size, size)), 0.0)


def column_of(row, eye):
    return jnp.sum(jnp.where(eye, jnp.broadcast_to(row, eye.shape), 0.0), axis=1, keepdims=True)


def eye_of(count):
    return (lax.broadcasted_iota(jnp.int32, (count, count), 0)
            == lax.broadcasted_iota(jnp.int32, (count, count), 1))


def widen(values, count):
    lane = lax.broadcasted_iota(jnp.int32, (1, count), 1)
    wide = count // len(values)
    out = jnp.zeros((1, count), F32)
    for j, value in enumerate(values):
        out = jnp.where((lane >= j * wide) & (lane < (j + 1) * wide), value, out)
    return out


def taper_of(position, where, mask, local_len):
    return mask * jnp.exp(-jnp.abs(position - where) / local_len)


def my_positions(rows, count, ncols):
    first = (lax.axis_index("row") * ncols + lax.axis_index("col")) * rows
    return (first + lax.broadcasted_iota(jnp.int32, (rows, count), 0)).astype(F32)


def gain_of(anom2, obs2, neg_inv2, taper, members):
    cross = dot3(anom2, obs2, NT) * (1.0 / (members - 1.0))
    return split2(dot3(split2(taper * cross), neg_inv2, NN))


def first_batch(nrows, ncols, g_ref, x_ref, rows_ref, owner_ref, mask_ref, val_ref, var_ref,
                inv_ref, x1_ref, anom_hi, anom_lo, push_hi, push_lo, aux_ref, rhs, beside):
    rows, members = x_ref.shape
    count = rows_ref.shape[1]
    nblk = mask_ref.shape[2]
    local_len = float(rows * nrows * ncols // 4)
    g0 = g_ref[0].reshape(count, members)
    m0 = row_mean(g0)
    a0 = g0 - m0
    anom_hi[...], anom_lo[...] = split2(a0)
    covariance((anom_hi[...], anom_lo[...]), var_ref[0:1, :], inv_ref)
    beside(0)
    lane = lax.broadcasted_iota(jnp.int32, (1, count), 1)
    device = jnp.zeros((1, count), jnp.int32)
    for c in range(1, ncols):
        device = device + jnp.where(lane >= c * (count // ncols), 1, 0)
    for b in range(2):
        aux_ref[b:b + 1, :] = ((owner_ref[b] * ncols + device) * rows + rows_ref[b:b + 1, :]).astype(F32)
        aux_ref[2 + b:3 + b, :] = widen([mask_ref[b, 0, j].astype(F32) for j in range(nblk)], count)
    aux_ref[4:6, :] = val_ref[...]
    aux_ref[6:8, :] = var_ref[...]
    push_hi[...], push_lo[...] = split2(column_of(val_ref[0:1, :], eye_of(count)) - m0 - 0.5 * a0)
    steps = count // W
    cuts = [0, steps // 4, 5 * steps // 8, steps]
    for k in range(3):
        sweep_inverse(inv_ref, rhs, cuts[k], cuts[k + 1])
        beside(k + 1)
    x = x_ref[...]
    taper = taper_of(my_positions(rows, count, ncols), aux_ref[0:1, :], aux_ref[2:3, :], local_len)
    gain = gain_of(split2(x - row_mean(x)), (anom_hi[...], anom_lo[...]), split2(inv_ref[...]), taper, members)
    x1_ref[...] = x - dot3(gain, (push_hi[...], push_lo[...]), NN)
    beside(5)


def solo_kernel(nrows, ncols, *refs):
    first_batch(nrows, ncols, *refs, lambda stage: None)


def flip(index, bits):
    bit = 1
    while bit <= bits:
        if bits & bit:
            index = index + bit - 2 * bit * ((index // bit) % 2)
        bit *= 2
    return index


def share_kernel(nrows, ncols, x_hbm, rows_hbm, owner_hbm, mask_hbm, val_hbm, var_hbm, g_ref, note_ref,
                 inv_ref, x1_ref, anom_hi, anom_lo, push_hi, push_lo, aux_ref,
                 rhs, x_ref, rows_ref, owner_ref, mask_ref, val_ref, var_ref, load, src, core_slot, part, slots,
                 note_src, note_slots, core_s, core_r, sum_s, sum_r, line_s, line_r, plane_s, plane_r, pair_s, pair_r,
                 nsum_s, nsum_r, nline_s, nline_r):
    loads = [pltpu.make_async_copy(source, target, load.at[k]) for k, (source, target) in enumerate((
        (x_hbm, x_ref), (rows_hbm, rows_ref), (owner_hbm, owner_ref), (mask_hbm, mask_ref),
        (val_hbm, val_ref), (var_hbm, var_ref)))]
    for copy in loads:
        copy.start()
    me = lax.axis_index("row")
    col = lax.axis_index("col")
    nstate, members = x_ref.shape
    count = rows_ref.shape[1]
    per_dev = count // ncols
    q = per_dev // nrows
    half = nrows // 2
    core = me % 2
    chip = me // 2
    sibling = flip(me, 1)
    beside_x = flip(me, 2)
    beside_y = flip(me, 4)
    across = flip(me, 6)
    cut = members // 2

    barrier = pltpu.get_barrier_semaphore()
    for d in range(1, nrows):
        pl.semaphore_signal(barrier, inc=1, device_id=(flip(me, d), col), device_id_type=MESH)
    for d in range(1, ncols):
        pl.semaphore_signal(barrier, inc=1, device_id=(me, flip(col, d)), device_id_type=MESH)

    sent = []

    def put(source, target, send, recv, row, column):
        copy = pltpu.make_async_remote_copy(
            src_ref=source, dst_ref=target, send_sem=send, recv_sem=recv,
            device_id=(row, column), device_id_type=MESH)
        copy.start()
        sent.append(copy)
        return copy

    def same(ref, send, recv, row):
        return put(ref, ref, send, recv, row, col)

    for copy in loads:
        copy.wait()
    x3 = split3(x_ref[...])
    state_ids = lax.broadcasted_iota(jnp.int32, (nstate, per_dev), 0)

    def select(b):
        ids = jnp.broadcast_to(rows_ref[b:b + 1, :], (8, count))
        ids = pltpu.roll(ids, (count - col * per_dev) % count, 1)[0:1, :per_dev]
        here = jnp.full((1, per_dev), owner_ref[b], jnp.int32) == me
        ids = jnp.where(here, ids, -1)
        pick = jnp.where(ids == state_ids, 1.0, 0.0).astype(BF16)
        rows = (mm(pick, x3[0], TN) + mm(pick, x3[1], TN)) + mm(pick, x3[2], TN)
        src[b] = rows.reshape(half, 2, q, members)

    def to_core(b):
        return put(src.at[b, :, 1 - core], core_slot.at[b], core_s.at[b], core_r.at[b], sibling, col)

    def to_chips(b, copy):
        copy.wait_recv()
        part[b] = src[b, :, core] + core_slot[b]
        return [put(part.at[b, flip(chip, d)], slots.at[b, d - 1], sum_s.at[b, d - 1], sum_r.at[b, d - 1],
                    flip(me, 2 * d), col) for d in range(1, half)]

    def along_line(b, copies):
        for copy in copies:
            copy.wait_recv()
        total = part[b, chip]
        for d in range(1, half):
            total = total + slots[b, d - 1]
        g_ref[b, col, me] = total
        mine = g_ref.at[b, col, me]
        return [put(mine, mine, line_s.at[b, d - 1], line_r.at[b, d - 1], me, flip(col, d))
                for d in range(1, ncols)]

    def spread(b, d):
        slab = g_ref.at[b, flip(col, d), me]
        x_copy = same(slab, plane_s.at[b, d, 0], plane_r.at[b, d, 0], beside_x)
        y_copy = same(slab, plane_s.at[b, d, 1], plane_r.at[b, d, 1], beside_y)
        return [x_copy, y_copy], [same(slab, pair_s.at[b, d, 0], pair_r.at[b, d, 0], sibling)]

    def spread_lines(b, lines, first):
        planes, pairs = [first[0]], list(first[1])
        for d in range(1, ncols):
            lines[d - 1].wait_recv()
            more = spread(b, d)
            planes.append(more[0])
            pairs.extend(more[1])
        return planes, pairs

    def relay(b, d, planes, pairs):
        planes[d][0].wait_recv()
        slab = g_ref.at[b, flip(col, d), beside_x]
        planes[d].append(same(slab.at[:, :cut], plane_s.at[b, d, 2], plane_r.at[b, d, 2], beside_y))
        pairs.append(same(slab, pair_s.at[b, d, 1], pair_r.at[b, d, 1], sibling))
        planes[d][1].wait_recv()
        slab = g_ref.at[b, flip(col, d), beside_y]
        planes[d].append(same(slab.at[:, cut:], plane_s.at[b, d, 3], plane_r.at[b, d, 3], beside_x))
        pairs.append(same(slab, pair_s.at[b, d, 2], pair_r.at[b, d, 2], sibling))

    def relay_all(b, planes, pairs):
        for d in range(ncols):
            relay(b, d, planes, pairs)

    def finish(b, planes, pairs):
        for d in range(ncols):
            planes[d][2].wait_recv()
            planes[d][3].wait_recv()
            pairs.append(same(g_ref.at[b, flip(col, d), across], pair_s.at[b, d, 3], pair_r.at[b, d, 3], sibling))

    lane = lax.broadcasted_iota(jnp.int32, (8, 128), 1)
    note = jnp.zeros((8, 128), F32)
    for j in range(mask_ref.shape[2]):
        note = jnp.where(lane == j, mask_ref[0, 0, j].astype(F32), note)
    here = jnp.full((8, 128), owner_ref[1], jnp.int32) == me
    note_src[...] = jnp.where(here, note, 0.0)
    select(0)
    pl.semaphore_wait(barrier, nrows + ncols - 2)
    core0 = to_core(0)
    select(1)
    core1 = to_core(1)
    sums0 = to_chips(0, core0)
    lines0 = along_line(0, sums0)
    first0 = spread(0, 0)
    sums1 = to_chips(1, core1)
    notes = [put(note_src, note_slots.at[d - 1], nsum_s.at[d - 1], nsum_r.at[d - 1], flip(me, d), col)
             for d in range(1, nrows)]
    planes0, pairs0 = spread_lines(0, lines0, first0)
    lines1 = along_line(1, sums1)
    later = [lines1, spread(1, 0)]
    relay_all(0, planes0, pairs0)
    finish(0, planes0, pairs0)
    total = note_src[...]
    for d in range(1, nrows):
        notes[d - 1].wait_recv()
        total = total + note_slots[d - 1]
    note_ref[col] = total
    note_lines = [put(note_ref.at[col], note_ref.at[col], nline_s.at[d - 1], nline_r.at[d - 1], me, flip(col, d))
                  for d in range(1, ncols)]
    for copy in pairs0:
        copy.wait_recv()

    def beside(stage):
        if stage == 0:
            later[:] = spread_lines(1, *later)
        elif stage == 1:
            relay_all(1, *later)
        elif stage == 2:
            finish(1, *later)
        elif stage == 5:
            for copy in later[1] + note_lines:
                copy.wait_recv()

    first_batch(nrows, ncols, g_ref, x_ref, rows_ref, owner_ref, mask_ref, val_ref, var_ref,
                inv_ref, x1_ref, anom_hi, anom_lo, push_hi, push_lo, aux_ref, rhs, beside)
    for copy in sent:
        copy.wait_send()


def second_kernel(nrows, ncols, nblk, g_ref, note_ref, inv_ref, x1_ref, anom_hi, anom_lo, push_hi, push_lo, aux_ref,
                  out_ref, g1, cov, rhs):
    rows, members = x1_ref.shape
    count = inv_ref.shape[0]
    local_len = float(rows * nrows * ncols // 4)
    eye = eye_of(count)
    mask_g = jnp.concatenate(
        [jnp.broadcast_to(widen([note_ref[c, 0:1, j:j + 1] for j in range(nblk)], count), (count // ncols, count))
         for c in range(ncols)], axis=0)
    taper = taper_of(column_of(aux_ref[1:2, :], eye), aux_ref[0:1, :], mask_g, local_len)
    g = g_ref[1].reshape(count, members)
    gain = gain_of(split2(g - row_mean(g)), (anom_hi[...], anom_lo[...]), split2(inv_ref[...]), taper, members)
    g1[...] = g - dot3(gain, (push_hi[...], push_lo[...]), NN)
    g = g1[...]
    m1 = row_mean(g)
    a1 = g - m1
    a12 = split2(a1)
    covariance(a12, aux_ref[7:8, :], cov)
    sweep_inverse(cov, rhs)
    push = split2(column_of(aux_ref[5:6, :], eye) - m1 - 0.5 * a1)
    x = x1_ref[...]
    taper = taper_of(my_positions(rows, count, ncols), aux_ref[1:2, :], aux_ref[3:4, :], local_len)
    gain = gain_of(split2(x - row_mean(x)), a12, split2(cov[...]), taper, members)
    out_ref[...] = x - dot3(gain, push, NN)


def shared_by_collectives(ensemble, obs_rows, owner, taper_mask, ncols):
    rows, members = ensemble.shape
    batches, count = obs_rows.shape
    per_dev = count // ncols
    nblk = taper_mask.shape[2]
    my_row = lax.axis_index("row")
    mine = lax.dynamic_slice_in_dim(obs_rows, lax.axis_index("col") * per_dev, per_dev, axis=1)
    row_ids = jnp.arange(rows, dtype=jnp.int32)
    shared = []
    for batch in range(batches):
        here = owner[batch] == my_row
        picker = ((mine[batch][:, None] == row_ids[None, :]) & here).astype(F32)
        part = jnp.dot(picker, ensemble, precision=lax.Precision.HIGHEST)
        shared.append(lax.all_gather(lax.psum(part, "row"), "col", axis=0).reshape(count, members))
    note = jnp.where(owner[1] == my_row, taper_mask[0, 0].astype(F32), 0.0)
    note = jnp.pad(jnp.broadcast_to(note[None, :], (8, nblk)), ((0, 0), (0, 128 - nblk)))
    note = lax.all_gather(lax.psum(note, "row"), "col", axis=0)
    return jnp.stack(shared), note


def on_device(nrows, ncols, ensemble, obs_rows, owner, obs_value, obs_var, taper_mask):
    rows, members = ensemble.shape
    batches, count = obs_rows.shape
    per_dev = count // ncols
    half_shape = jax.ShapeDtypeStruct((count, members), BF16)
    kept = (
        jax.ShapeDtypeStruct((count, count), F32),
        jax.ShapeDtypeStruct((rows, members), F32),
        half_shape, half_shape, half_shape, half_shape,
        jax.ShapeDtypeStruct((8, count), F32),
    )
    limit = 40 * 2**20
    terms = [pltpu.VMEM((3, 128, count), BF16)]
    if nrows == 8 and ncols & (ncols - 1) == 0 and per_dev % (8 * nrows) == 0:
        q = per_dev // nrows
        half = nrows // 2
        dma = pltpu.SemaphoreType.DMA
        shared, note, *held = pl.pallas_call(
            functools.partial(share_kernel, nrows, ncols),
            out_shape=(
                jax.ShapeDtypeStruct((batches, ncols, nrows, q, members), F32),
                jax.ShapeDtypeStruct((ncols, 8, 128), F32),
            ) + kept,
            in_specs=[HBM] * 6,
            out_specs=(VMEM,) * 9,
            scratch_shapes=terms + [
                pltpu.VMEM(ensemble.shape, F32),
                pltpu.VMEM(obs_rows.shape, jnp.int32),
                pltpu.SMEM(owner.shape, jnp.int32),
                pltpu.SMEM(taper_mask.shape, jnp.int32),
                pltpu.VMEM(obs_value.shape, F32),
                pltpu.VMEM(obs_var.shape, F32),
                dma((6,)),
                pltpu.VMEM((batches, half, 2, q, members), F32),
                pltpu.VMEM((batches, half, q, members), F32),
                pltpu.VMEM((batches, half, q, members), F32),
                pltpu.VMEM((batches, half - 1, q, members), F32),
                pltpu.VMEM((8, 128), F32),
                pltpu.VMEM((nrows - 1, 8, 128), F32),
            ] + [dma((batches,))] * 2 + [dma((batches, half - 1))] * 2 + [dma((batches, ncols - 1))] * 2
            + [dma((batches, ncols, 4))] * 4 + [dma((nrows - 1,))] * 2 + [dma((ncols - 1,))] * 2,
            compiler_params=pltpu.CompilerParams(
                vmem_limit_bytes=limit, collective_id=0, has_side_effects=True),
        )(*[pltpu.with_memory_space_constraint(arg, pltpu.HBM)
            for arg in (ensemble, obs_rows, owner, taper_mask, obs_value, obs_var)])
    else:
        shared, note = shared_by_collectives(ensemble, obs_rows, owner, taper_mask, ncols)
        held = pl.pallas_call(
            functools.partial(solo_kernel, nrows, ncols),
            out_shape=kept,
            in_specs=[VMEM] * 3 + [SMEM] * 2 + [VMEM] * 2,
            out_specs=(VMEM,) * 7,
            scratch_shapes=terms,
            compiler_params=pltpu.CompilerParams(vmem_limit_bytes=limit),
        )(shared, ensemble, obs_rows, owner, taper_mask, obs_value, obs_var)
    return pl.pallas_call(
        functools.partial(second_kernel, nrows, ncols, taper_mask.shape[2]),
        out_shape=jax.ShapeDtypeStruct((rows, members), F32),
        in_specs=[VMEM] * 9,
        out_specs=VMEM,
        scratch_shapes=[pltpu.VMEM((count, members), F32), pltpu.VMEM((count, count), F32)] + terms,
        compiler_params=pltpu.CompilerParams(vmem_limit_bytes=limit),
    )(shared, note, *held)


def solution(mesh):
    in_specs = (P(("row", "col"), None), P(), P(), P(), P(), P(None, ("row", "col"), None))
    out_specs = P(("row", "col"), None)
    return jax.shard_map(
        functools.partial(on_device, mesh.shape["row"], mesh.shape["col"]),
        mesh=mesh, in_specs=in_specs, out_specs=out_specs, check_vma=False
    )
```
